32 devices in a mesh: queue: 4 (over y, core), seq: 8 (over z, x).
Axes of the slice: x: 2, y: 2, z: 4, core: 2. Of those that a mesh axis runs over, the one named last changes fastest.
Arguments:
- latents: float32 [16, 16, 1024], P('queue', None, 'seq'), may hold values from -6 to 6
- step_index: int32 [16], P('queue'), may hold values from 0 to 29, as said below
- levels: float32 [31], replicated, may hold values from 0 to 1, as said below
- modulation: float32 [30, 5, 1152], replicated, may hold values from -4 to 4
- embed_weight: bfloat16 [16, 1152], replicated, may hold values from -1.5 to 1.5
- position: bfloat16 [1024, 1152], P('seq'), may hold values from -3 to 3
- qkv_weight: bfloat16 [1152, 3456], replicated, may hold values from -0.1875 to 0.1875
- q_gain: float32 [72], replicated, may hold values from 1 to 2.5
- k_gain: float32 [72], replicated, may hold values from 1 to 2.5
- text_kv: bfloat16 [2, 128, 1152], P(None, None, 'seq'), may hold values from -6 to 6
- out_weight: bfloat16 [1152, 1152], replicated, may hold values from -0.1875 to 0.1875
- final_weight: bfloat16 [1152, 16], replicated, may hold values from -0.1875 to 0.1875
- new_noise: float32 [16, 1024], P(None, 'seq'), may hold values from -6 to 6
Outputs:
- advanced: float32 [16, 16, 1024], P('queue', None, 'seq')
- velocity: float32 [16, 16, 1024], P('queue', None, 'seq')
The draws below stay inside these ranges and needn't reach their ends.
Inputs may be any that keep to these rules, and one draw needn't show every extreme that they name: `step_index`: frame 0 has index 0 and the last frame 30 - 1; frame j otherwise has j * 30 // 16 or one more, at most 29. levels rise strictly from exactly 0 at index 0 to exactly 1 at index 30.
All inputs are finite; a program needn't handle non-finite values.
Results may differ from the reference program's by a relative error of at most 0.0044.
Values may be sent and summed in bfloat16 or wider, within the bound.
No kernel may reach another device: no remote copies, remote signals or barrier semaphores. Data moves between devices by JAX's collectives and lax.ppermute only.
A program may use at most 128 MiB of HBM per device.

```python
import math
import jax
import jax.numpy as jnp
from jax import lax

D = 1152
HEADS = 16
HD = 72
C = 16
TXT = 128
STEPS = 30
FRAMES = 16
TOKENS = 1024


def draw_step_index(key, part):
    places = jnp.arange(FRAMES, dtype=jnp.int32)
    base_index = places * STEPS // FRAMES
    jitter = jax.random.randint(key, (FRAMES,), 0, 2, dtype=jnp.int32)
    chosen = jnp.clip(base_index + jitter, 0, STEPS - 1)
    chosen = jnp.where(places == 0, 0, chosen)
    chosen = jnp.where(places == FRAMES - 1, STEPS - 1, chosen)
    return chosen.astype(jnp.int32)


def draw_levels(key, part):
    increments = jax.random.uniform(key, (STEPS,), jnp.float32, 0.3, 1.7)
    rising = jnp.concatenate([jnp.zeros((1,), jnp.float32), jnp.cumsum(increments)]) / jnp.sum(increments)
    places = jnp.arange(STEPS + 1)
    return jnp.where(places == STEPS, 1.0, rising).astype(jnp.float32)


def block_levels(own_key, dims, pieces, least, top_value):
    def one(dim, parts):
        steps = jax.random.uniform(jax.random.fold_in(jax.random.fold_in(own_key, 6), dim), (parts,), jnp.float32, least / len(pieces), top_value / len(pieces))
        return jnp.repeat(jnp.exp(steps), dims[dim] // parts).reshape((-1,) + (1,) * (len(dims) - dim - 1))

    factor_of = one(*pieces[0])
    for cut in pieces[1:]:
        factor_of = factor_of * one(*cut)
    return factor_of


def gaussian(own_key, extent, spread, reach, shards=(), kind=jnp.bfloat16):
    result = jax.random.normal(own_key, extent, jnp.float32) * spread
    if len(shards) > 0:
        result = block_levels(own_key, extent, shards, -0.22, 0.18) * result
    return jnp.clip(result, min=-reach, max=reach).astype(kind)


def setup_inputs(seed: int = 0) -> dict:
    splits = jax.random.split(jax.random.key(seed), 14)
    latents = gaussian(splits[0], (FRAMES, C, TOKENS), 1.0, 6.0, ((0, 4), (2, 8)), jnp.float32)
    step_index = draw_step_index(jax.random.fold_in(splits[13], 71), 0)
    levels = draw_levels(jax.random.fold_in(splits[13], 71), 0)
    modulation = gaussian(splits[3], (STEPS, 5, D), 0.5, 4.0, (), jnp.float32)
    embed_weight = gaussian(splits[4], (C, D), C ** -0.5, 1.5)
    position = gaussian(splits[5], (TOKENS, D), 0.5, 3.0, ((0, 8),))
    qkv_weight = gaussian(splits[6], (D, 3 * D), D ** -0.5, 0.1875)
    q_gain = jnp.clip(jnp.exp(jax.random.uniform(splits[7], (HD,), jnp.float32, math.log(1.0), math.log(2.5))), 1.0, 2.5)
    k_gain = jnp.clip(jnp.exp(jax.random.uniform(splits[8], (HD,), jnp.float32, math.log(1.0), math.log(2.5))), 1.0, 2.5)
    text_kv = gaussian(splits[9], (2, TXT, D), 1.0, 6.0, ((2, 8),))
    out_weight = gaussian(splits[10], (D, D), D ** -0.5, 0.1875)
    final_weight = gaussian(splits[11], (D, C), D ** -0.5, 0.1875)
    new_noise = gaussian(splits[12], (C, TOKENS), 1.0, 6.0, ((1, 8),), jnp.float32)
    return {"latents": latents, "step_index": step_index, "levels": levels, "modulation": modulation, "embed_weight": embed_weight, "position": position, "qkv_weight": qkv_weight, "q_gain": q_gain, "k_gain": k_gain, "text_kv": text_kv, "out_weight": out_weight, "final_weight": final_weight, "new_noise": new_noise}


EPSILON = 1e-06

def layer_norm(values):
    center = values - lax.optimization_barrier(jnp.mean(values, axis=-1, keepdims=True))
    return center * lax.rsqrt(lax.optimization_barrier(jnp.mean(center * center, axis=-1, keepdims=True)) + EPSILON)

def head_norm(values, gain_vector):
    widened = values.astype(jnp.float32)
    scaled = widened * lax.rsqrt(lax.optimization_barrier(jnp.mean(widened * widened, axis=-1, keepdims=True)) + EPSILON) * gain_vector
    return scaled.astype(jnp.bfloat16)

def attend_one(head_args):
    queries, keys_all, values_all, text_keys, text_values = head_args
    factor = 1.0 / math.sqrt(queries.shape[-1])
    scores = jnp.dot(queries, keys_all.T, preferred_element_type=jnp.float32) * factor
    weights = jnp.exp(scores)
    numerator = jnp.dot(weights.astype(jnp.bfloat16), values_all, preferred_element_type=jnp.float32)
    own_part = numerator / lax.optimization_barrier(jnp.sum(weights, axis=-1, keepdims=True))
    text_scores = jnp.dot(queries, text_keys.T, preferred_element_type=jnp.float32) * factor
    text_weights = jnp.exp(text_scores)
    text_numerator = jnp.dot(text_weights.astype(jnp.bfloat16), text_values, preferred_element_type=jnp.float32)
    return own_part + text_numerator / lax.optimization_barrier(jnp.sum(text_weights, axis=-1, keepdims=True))

def reference(latents, step_index, levels, modulation, embed_weight, position, qkv_weight, q_gain, k_gain, text_kv, out_weight, final_weight, new_noise):
    highest = lax.Precision.HIGHEST
    select = (step_index[:, None] == jnp.arange(STEPS, dtype=jnp.int32)[None, :]).astype(jnp.float32)
    frame_mods = jnp.dot(select, modulation.reshape(STEPS, 5 * D), precision=highest).reshape(FRAMES, 5, 1, D)
    level_low = jnp.dot(select, levels[:STEPS], precision=highest)
    level_high = jnp.dot(select, levels[1:], precision=highest)
    hidden = jnp.einsum('fcn,cd->fnd', latents, embed_weight.astype(jnp.float32), precision=highest)
    hidden = hidden + position.astype(jnp.float32)[None]
    normed = (layer_norm(hidden) * (1.0 + frame_mods[:, 1]) + frame_mods[:, 0]).astype(jnp.bfloat16)
    projected = jnp.dot(normed.reshape(FRAMES * TOKENS, D), qkv_weight, preferred_element_type=jnp.float32)
    projected = projected.astype(jnp.bfloat16).reshape(FRAMES, TOKENS, 3, HEADS, HD)
    query_heads = jnp.moveaxis(head_norm(projected[:, :, 0], q_gain), 2, 1)
    key_heads = jnp.moveaxis(head_norm(projected[:, :, 1], k_gain), 2, 1)
    value_heads = jnp.moveaxis(projected[:, :, 2], 2, 1)
    text_keys = jnp.moveaxis(head_norm(text_kv[0].reshape(TXT, HEADS, HD), k_gain), 1, 0)
    text_values = jnp.moveaxis(text_kv[1].reshape(TXT, HEADS, HD), 1, 0)

    def per_frame(frame_args):
        frame_q, frame_k, frame_v = frame_args
        return lax.map(attend_one, (frame_q, frame_k, frame_v, text_keys, text_values))
    mixture = lax.map(per_frame, (query_heads, key_heads, value_heads))
    attention = jnp.moveaxis(mixture, 1, 2).reshape(FRAMES, TOKENS, D).astype(jnp.bfloat16)
    branch = jnp.dot(attention.reshape(FRAMES * TOKENS, D), out_weight, preferred_element_type=jnp.float32).reshape(FRAMES, TOKENS, D)
    hidden_two = hidden + frame_mods[:, 2] * branch
    normed_two = (layer_norm(hidden_two) * (1.0 + frame_mods[:, 4]) + frame_mods[:, 3]).astype(jnp.bfloat16)
    velocity = jnp.einsum('fnd,dc->fcn', normed_two.astype(jnp.float32), final_weight.astype(jnp.float32))
    updated = latents + velocity * (level_high - level_low)[:, None, None]
    advanced = jnp.concatenate([updated[1:], new_noise[None]], axis=0)
    return (advanced, velocity)
```

```python
import functools
import math

import jax
import jax.numpy as jnp
from jax import lax
from jax.experimental import pallas as pl
from jax.experimental.pallas import tpu as pltpu
from jax.sharding import PartitionSpec as P

EPSILON = 1e-06
LANES = 128
ROWS = 16
F32 = jnp.float32
BF16 = jnp.bfloat16
VMEM_LIMIT = 56 * 1024 * 1024
NT = (((1,), (1,)), ((), ()))
TN = (((0,), (0,)), ((), ()))


def dot(a, b, dims=(((1,), (0,)), ((), ()))):
    return lax.dot_general(a, b, dims, preferred_element_type=F32)


def split_parts(values):
    high = values.astype(BF16)
    low = (values - high.astype(F32)).astype(BF16)
    return high, low


def prep_kernel(frames, share, position_ref, latents_ref, *payload_refs):
    tokens, width = position_ref.shape
    half = tokens // 2
    pieces = half // ROWS
    core = lax.rem(lax.axis_index("queue"), 2)
    own_frame = lax.div(lax.axis_index("seq"), share)
    for piece in range(pieces):
        start = pl.multiple_of(core * half + piece * ROWS, ROWS)
        rows = position_ref[pl.ds(start, ROWS), :]
        for payload_ref in payload_refs:
            payload_ref[:, piece * width : (piece + 1) * width] = rows
    for d, payload_ref in enumerate(payload_refs):
        values = latents_ref[jnp.bitwise_xor(own_frame, d)]
        high, low = split_parts(values)
        base = pieces * width
        payload_ref[:, base : base + tokens] = high
        payload_ref[:, base + tokens : base + 2 * tokens] = low


def prep(position, latents, frames, share):
    tokens, width = position.shape
    columns = tokens // 2 // ROWS * width + 2 * tokens
    return pl.pallas_call(
        functools.partial(prep_kernel, frames, share),
        out_shape=[jax.ShapeDtypeStruct((ROWS, columns), BF16)] * frames,
        name="prep",
    )(position, latents)


def unpack(block, mine_ref, other_ref, position_scr, latents_scr, width, tokens):
    half = tokens // 2
    pieces = half // ROWS
    core = lax.rem(lax.axis_index("queue"), 2)
    for ref, place in ((mine_ref, core), (other_ref, 1 - core)):
        for piece in range(pieces):
            start = pl.multiple_of(block * tokens + place * half + piece * ROWS, ROWS)
            position_scr[pl.ds(start, ROWS), :] = ref[:, piece * width : (piece + 1) * width]
    base = pieces * width
    latents_scr[block, 0:ROWS, :] = mine_ref[:, base : base + tokens]
    latents_scr[block, ROWS : 2 * ROWS, :] = mine_ref[:, base + tokens : base + 2 * tokens]


def normalize(values, scale, shift):
    center = values - jnp.mean(values, axis=-1, keepdims=True)
    variance = jnp.mean(center * center, axis=-1, keepdims=True)
    return (center * lax.rsqrt(variance + EPSILON) * scale + shift).astype(BF16)


def embed_blocks(blocks, position_scr, latents_scr, embed_ref, mods_ref, normed_scr, hidden_ref):
    tokens = latents_scr.shape[2]
    embed = jnp.concatenate([embed_ref[...], embed_ref[...]], axis=0)
    scale = 1.0 + mods_ref[1:2, :]
    shift = mods_ref[0:1, :]

    def one(block, carry):
        rows = pl.ds(pl.multiple_of(block * tokens, tokens), tokens)
        hidden = dot(latents_scr[block], embed, TN) + position_scr[rows, :].astype(F32)
        if hidden_ref is not None:
            hidden_ref[rows, :] = hidden
        normed_scr[rows, :] = normalize(hidden, scale, shift)
        return carry

    lax.fori_loop(0, blocks, one, 0)


def head_sums(width, head):
    column = lax.broadcasted_iota(jnp.int32, (width, LANES), 0)
    first = lax.broadcasted_iota(jnp.int32, (width, LANES), 1) * head
    return jnp.where((column >= first) & (column < first + head), 1.0, 0.0).astype(BF16)


def head_spread(width, head):
    column = lax.broadcasted_iota(jnp.int32, (LANES, width), 1)
    first = lax.broadcasted_iota(jnp.int32, (LANES, width), 0) * head
    one = jnp.where((column >= first) & (column < first + head), 1.0, 0.0).astype(BF16)
    return jnp.concatenate([one, one], axis=0)


def spread(values, spread_matrix):
    high, low = split_parts(values)
    return dot(jnp.concatenate([high, low], axis=1), spread_matrix)


def head_norm(values, gain, head, sums_matrix, spread_matrix):
    wide = values.astype(F32)
    squares = dot((wide * wide).astype(BF16), sums_matrix) * (1.0 / head)
    factor = spread(lax.rsqrt(squares + EPSILON), spread_matrix)
    return (wide * factor * gain).astype(BF16)


def project(normed_scr, weight_ref, first, last, out_ref, chunk=256):
    for start in range(first, last, chunk):
        end = min(start + chunk, last)
        out_ref[:, start - first : end - first] = dot(
            normed_scr[...], weight_ref[:, start:end]
        ).astype(BF16)


def norm_rows(source, columns, target, gain, head, sums_matrix, spread_matrix, step=128):
    def one(i, carry):
        rows = pl.ds(pl.multiple_of(i * step, step), step)
        target[rows, :] = head_norm(
            source[rows, columns], gain, head, sums_matrix, spread_matrix
        )
        return carry

    lax.fori_loop(0, target.shape[0] // step, one, 0)


def window(first, last, width):
    start = first // LANES * LANES
    end = min(-(-last // LANES) * LANES, width)
    return start, end


def lane_mask(shape, first, last):
    lane = lax.broadcasted_iota(jnp.int32, shape, 1)
    return (lane >= first) & (lane < last)


def keep(values, first, last):
    return jnp.where(lane_mask(values.shape, first, last), values, jnp.zeros_like(values))


def attend_self(q_ref, k_scr, v_ref, v_base, num_ref, sum_ref, head, heads, fresh, q_step):
    queries, width = q_ref.shape
    keys = k_scr.shape[0]

    def tile(i, carry):
        rows = pl.ds(pl.multiple_of(i * q_step, q_step), q_step)
        sums = jnp.zeros((q_step, LANES), F32)
        for h in range(heads):
            first, last = h * head, (h + 1) * head
            start, end = window(first, last, width)
            in_first, in_last = first - start, last - start
            q = keep(q_ref[rows, start:end], in_first, in_last)
            scores = dot(q, k_scr[:, start:end], NT)
            weights = jnp.exp2(scores).astype(BF16)
            v = keep(v_ref[:, v_base + start : v_base + end], in_first, in_last)
            mark = lane_mask((keys, LANES), h, h + 1)
            if end - start == LANES:
                ones = jnp.where(mark, 1.0, 0.0).astype(BF16)
                both = dot(weights, jnp.concatenate([v, ones], axis=1))
                sums = sums + both[:, LANES:]
                num_ref[rows, start:end] += both[:, :LANES]
            else:
                lead = jnp.where(mark, jnp.ones((), BF16), v[:, :LANES])
                both = dot(weights, jnp.concatenate([lead, v[:, LANES:]], axis=1))
                tops = lane_mask((q_step, LANES), 0, heads)
                left = both[:, :LANES]
                sums = sums + jnp.where(tops, left, 0.0)
                num_ref[rows, start : start + LANES] += jnp.where(tops, 0.0, left)
                num_ref[rows, start + LANES : end] += both[:, LANES:]
        sum_ref[rows, :] += sums
        return carry

    lax.fori_loop(0, queries // q_step, tile, 0)


def attend_text(q_ref, tk_scr, tv_scr, num_ref, sum_ref, head, heads, q_step):
    queries, width = q_ref.shape
    keys = tk_scr.shape[0]

    def tile(i, carry):
        rows = pl.ds(pl.multiple_of(i * q_step, q_step), q_step)
        sums = jnp.zeros((q_step, LANES), F32)
        for pair in range(0, heads, 2):
            first, middle, last = pair * head, (pair + 1) * head, (pair + 2) * head
            start, end = window(first, last, width)
            spans = ((first - start, middle - start), (middle - start, last - start))
            k = jnp.concatenate([keep(tk_scr[:, start:end], *span) for span in spans], axis=0)
            v = jnp.concatenate([keep(tv_scr[:, start:end], *span) for span in spans], axis=0)
            ones = jnp.concatenate(
                [
                    jnp.where(lane_mask((keys, LANES), h, h + 1), 1.0, 0.0).astype(BF16)
                    for h in (pair, pair + 1)
                ],
                axis=0,
            )
            weights = jnp.exp2(dot(q_ref[rows, start:end], k, NT)).astype(BF16)
            num_ref[rows, start:end] += dot(weights, v)
            sums = sums + dot(weights, ones)
        sum_ref[rows, :] = sums
        return carry

    lax.fori_loop(0, queries // q_step, tile, 0)


def own_kernel(
    frames, head, heads, *refs
):
    mine = refs[:frames]
    other = refs[frames : 2 * frames]
    (embed_ref, mods_ref, weight_ref, gains_ref, q_ref, hidden_ref, num_ref, sum_ref) = refs[
        2 * frames : 2 * frames + 8
    ]
    position_scr, latents_scr, normed_scr, proj_scr, k_scr = refs[2 * frames + 8 :]
    width = embed_ref.shape[1]
    tokens = latents_scr.shape[2]
    for block in range(frames):
        unpack(block, mine[block], other[block], position_scr, latents_scr, width, tokens)
    embed_blocks(
        frames, position_scr, latents_scr, embed_ref, mods_ref, normed_scr, hidden_ref
    )
    project(normed_scr, weight_ref, 0, 3 * width, proj_scr)
    sums_matrix = head_sums(width, head)
    spread_matrix = head_spread(width, head)
    norm_rows(
        proj_scr, slice(0, width), q_ref, gains_ref[0:1, :], head, sums_matrix, spread_matrix
    )
    norm_rows(
        proj_scr,
        slice(width, 2 * width),
        k_scr,
        gains_ref[1:2, :],
        head,
        sums_matrix,
        spread_matrix,
    )
    num_ref[...] = jnp.zeros_like(num_ref)
    sum_ref[...] = jnp.zeros_like(sum_ref)
    attend_self(q_ref, k_scr, proj_scr, 2 * width, num_ref, sum_ref, head, heads, True, 256)


def rest_kernel(frames, head, heads, columns, *refs):
    count = frames * columns
    mine = refs[:count]
    other = refs[count : 2 * count]
    (
        embed_ref,
        mods_ref,
        weight_ref,
        gains_ref,
        q_ref,
        hidden_ref,
        num_in_ref,
        sum_in_ref,
        text_ref,
        out_weight_ref,
        final_weight_ref,
    ) = refs[2 * count : 2 * count + 11]
    velocity_refs = refs[2 * count + 11 : 2 * count + 11 + frames]
    (
        position_scr,
        latents_scr,
        normed_scr,
        proj_scr,
        k_scr,
        num_ref,
        sum_ref,
        tk_scr,
        tv_scr,
        tnum_scr,
        tsum_scr,
        attention_scr,
    ) = refs[2 * count + 11 + frames :]
    width = embed_ref.shape[1]
    tokens = latents_scr.shape[2]
    sums_matrix = head_sums(width, head)
    spread_matrix = head_spread(width, head)
    num_ref[...] = num_in_ref[...]
    sum_ref[...] = sum_in_ref[...]
    for column in range(columns):
        for block in range(frames):
            index = column * frames + block
            unpack(block, mine[index], other[index], position_scr, latents_scr, width, tokens)
        embed_blocks(frames, position_scr, latents_scr, embed_ref, mods_ref, normed_scr, None)
        project(normed_scr, weight_ref, width, 3 * width, proj_scr)
        norm_rows(
            proj_scr,
            slice(0, width),
            k_scr,
            gains_ref[1:2, :],
            head,
            sums_matrix,
            spread_matrix,
        )
        attend_self(q_ref, k_scr, proj_scr, width, num_ref, sum_ref, head, heads, False, 256)

    shards, _, text_len, part = text_ref.shape
    for shard in range(shards):
        tk_scr[:, shard * part : (shard + 1) * part] = text_ref[shard, 0]
        tv_scr[:, shard * part : (shard + 1) * part] = text_ref[shard, 1]
    norm_rows(
        tk_scr, slice(0, width), tk_scr, gains_ref[1:2, :], head, sums_matrix, spread_matrix
    )
    tnum_scr[...] = jnp.zeros_like(tnum_scr)
    attend_text(q_ref, tk_scr, tv_scr, tnum_scr, tsum_scr, head, heads, 256)

    def mix(i, carry):
        rows = pl.ds(pl.multiple_of(i * LANES, LANES), LANES)
        used = lane_mask((LANES, LANES), 0, heads)
        own = spread(jnp.where(used, 1.0 / sum_ref[rows, :], 0.0), spread_matrix)
        text = spread(jnp.where(used, 1.0 / tsum_scr[rows, :], 0.0), spread_matrix)
        attention_scr[rows, :] = (
            num_ref[rows, :] * own + tnum_scr[rows, :] * text
        ).astype(BF16)
        return carry

    lax.fori_loop(0, q_ref.shape[0] // LANES, mix, 0)
    num_ref[...] = dot(attention_scr[...], out_weight_ref[...])
    gate = mods_ref[2:3, :]
    shift = mods_ref[3:4, :]
    scale = 1.0 + mods_ref[4:5, :]
    for block in range(frames):
        rows = slice(block * tokens, (block + 1) * tokens)
        hidden = hidden_ref[rows, :] + gate * num_ref[rows, :]
        normed = normalize(hidden, scale, shift)
        velocity_refs[block][...] = dot(
            final_weight_ref[...], normed, (((0,), (1,)), ((), ()))
        )


def finish_kernel(
    frames,
    share,
    step_ref,
    levels_ref,
    latents_ref,
    *refs,
):
    arrived = refs[:frames]
    velocity_ref, moved_ref, first_ref = refs[frames:]
    own_frame = lax.div(lax.axis_index("seq"), share)
    for d in range(frames):
        frame = jnp.bitwise_xor(own_frame, d)
        velocity_ref[frame] = arrived[d][...]
    for frame in range(frames):
        index = step_ref[frame]
        size = levels_ref[index + 1] - levels_ref[index]
        updated = latents_ref[frame] + size * velocity_ref[frame]
        if frame == 0:
            first_ref[...] = updated
        else:
            moved_ref[frame - 1] = updated
    moved_ref[frames - 1] = jnp.zeros_like(first_ref)


def vmem(count):
    return [pl.BlockSpec(memory_space=pltpu.VMEM)] * count


def body(
    latents,
    step_index,
    levels,
    modulation,
    embed_weight,
    position,
    qkv_weight,
    q_gain,
    k_gain,
    text_kv,
    out_weight,
    final_weight,
    new_noise,
):
    frames, channels, tokens = latents.shape
    width = embed_weight.shape[1]
    head = q_gain.shape[0]
    heads = width // head
    seq = lax.axis_size("seq")
    queue = lax.axis_size("queue")
    share = seq // frames
    queries = frames * tokens
    own_frame = lax.axis_index("seq") // share

    def over_frames(value, d):
        return lax.ppermute(value, "seq", [(i, i ^ (d * share)) for i in range(seq)])

    def over_columns(value, d):
        return lax.ppermute(value, "seq", [(i, i ^ d) for i in range(seq)])

    def over_cores(value):
        return lax.ppermute(value, "queue", [(i, i ^ 1) for i in range(queue)])

    text = lax.all_gather(text_kv, "seq", axis=0, tiled=False)
    index = lax.dynamic_index_in_dim(step_index, own_frame, 0, keepdims=False)
    mods = lax.dynamic_index_in_dim(modulation, index, 0, keepdims=False)
    factor = math.log2(math.e) / math.sqrt(head)
    gains = jnp.stack([jnp.tile(q_gain * factor, heads), jnp.tile(k_gain, heads)])

    sent = prep(position, latents, frames, share)
    mine = [sent[0]] + [over_frames(sent[d], d) for d in range(1, frames)]
    other = [over_cores(value) for value in mine]
    columns = share - 1
    mine_far = [over_columns(value, d) for d in range(1, share) for value in mine]
    other_far = [over_cores(value) for value in mine_far]

    params = pltpu.CompilerParams(vmem_limit_bytes=VMEM_LIMIT)
    blocks = [
        pltpu.VMEM((queries, width), BF16),
        pltpu.VMEM((frames, 2 * channels, tokens), BF16),
        pltpu.VMEM((queries, width), BF16),
    ]
    q_hat, hidden, num, sums = pl.pallas_call(
        functools.partial(own_kernel, frames, head, heads),
        out_shape=[
            jax.ShapeDtypeStruct((queries, width), BF16),
            jax.ShapeDtypeStruct((queries, width), F32),
            jax.ShapeDtypeStruct((queries, width), F32),
            jax.ShapeDtypeStruct((queries, LANES), F32),
        ],
        in_specs=vmem(2 * frames + 4),
        out_specs=vmem(4),
        scratch_shapes=blocks
        + [pltpu.VMEM((queries, 3 * width), BF16), pltpu.VMEM((queries, width), BF16)],
        compiler_params=params,
        name="own_column",
    )(*mine, *other, embed_weight, mods, qkv_weight, gains)

    text_len = text.shape[2]
    velocities = pl.pallas_call(
        functools.partial(rest_kernel, frames, head, heads, columns),
        out_shape=[jax.ShapeDtypeStruct((channels, tokens), F32)] * frames,
        in_specs=vmem(2 * frames * columns + 11),
        out_specs=vmem(frames),
        scratch_shapes=blocks
        + [
            pltpu.VMEM((queries, 2 * width), BF16),
            pltpu.VMEM((queries, width), BF16),
            pltpu.VMEM((queries, width), F32),
            pltpu.VMEM((queries, LANES), F32),
            pltpu.VMEM((text_len, width), BF16),
            pltpu.VMEM((text_len, width), BF16),
            pltpu.VMEM((queries, width), F32),
            pltpu.VMEM((queries, LANES), F32),
            pltpu.VMEM((queries, width), BF16),
        ],
        compiler_params=params,
        name="rest",
    )(
        *mine_far,
        *other_far,
        embed_weight,
        mods,
        qkv_weight,
        gains,
        q_hat,
        hidden,
        num,
        sums,
        text,
        out_weight,
        final_weight,
    )

    arrived = [velocities[0]] + [over_frames(velocities[d], d) for d in range(1, frames)]
    smem = pl.BlockSpec(memory_space=pltpu.SMEM)
    velocity, moved, first = pl.pallas_call(
        functools.partial(finish_kernel, frames, share),
        out_shape=[
            jax.ShapeDtypeStruct((frames, channels, tokens), F32),
            jax.ShapeDtypeStruct((frames, channels, tokens), F32),
            jax.ShapeDtypeStruct((channels, tokens), F32),
        ],
        in_specs=[smem, smem] + vmem(frames + 1),
        out_specs=vmem(3),
        name="finish",
    )(step_index, levels, latents, *arrived)
    came = lax.ppermute(first, "queue", [(i, i - 1) for i in range(1, queue)])
    at_end = lax.axis_index("queue") == queue - 1
    came = jnp.where(at_end, new_noise, came)
    advanced = lax.dynamic_update_slice_in_dim(moved, came[None], frames - 1, 0)
    return (advanced, velocity)


def solution(mesh):
    in_specs = (
        P("queue", None, "seq"),
        P("queue"),
        P(),
        P(),
        P(),
        P("seq", None),
        P(),
        P(),
        P(),
        P(None, None, "seq"),
        P(),
        P(),
        P(None, "seq"),
    )
    out_specs = (P("queue", None, "seq"), P("queue", None, "seq"))
    return jax.shard_map(body, mesh=mesh, in_specs=in_specs, out_specs=out_specs, check_vma=False)
```

```python
import functools
import math

import jax
import jax.numpy as jnp
from jax import lax
from jax.experimental import pallas as pl
from jax.experimental.pallas import tpu as pltpu
from jax.sharding import PartitionSpec as P

EPSILON = 1e-06
LANES = 128
ROWS = 16
F32 = jnp.float32
BF16 = jnp.bfloat16
VMEM_LIMIT = 32 * 1024 * 1024
NT = (((1,), (1,)), ((), ()))
TN = (((0,), (0,)), ((), ()))


def dot(a, b, dims=(((1,), (0,)), ((), ()))):
    return lax.dot_general(a, b, dims, preferred_element_type=F32)


def split_parts(values):
    high = values.astype(BF16)
    low = (values - high.astype(F32)).astype(BF16)
    return high, low


def prep_kernel(frames, share, position_ref, latents_ref, text_ref, *payload_refs):
    tokens, width = position_ref.shape
    _, text_len, part = text_ref.shape
    half = tokens // 2
    pieces = half // ROWS
    core = lax.rem(lax.axis_index("queue"), 2)
    own_frame = lax.div(lax.axis_index("seq"), share)
    for piece in range(pieces):
        start = pl.multiple_of(core * half + piece * ROWS, ROWS)
        rows = position_ref[pl.ds(start, ROWS), :]
        for payload_ref in payload_refs:
            payload_ref[:, piece * width : (piece + 1) * width] = rows
    for d, payload_ref in enumerate(payload_refs):
        values = latents_ref[jnp.bitwise_xor(own_frame, d)]
        high, low = split_parts(values)
        base = pieces * width
        payload_ref[:, base : base + tokens] = high
        payload_ref[:, base + tokens : base + 2 * tokens] = low
    base = pieces * width + 2 * tokens
    for piece in range(text_len // ROWS):
        rows = text_ref[core, piece * ROWS : (piece + 1) * ROWS, :]
        for payload_ref in payload_refs:
            payload_ref[:, base + piece * part : base + (piece + 1) * part] = rows


def prep(position, latents, text_kv, frames, share):
    tokens, width = position.shape
    _, text_len, part = text_kv.shape
    columns = tokens // 2 // ROWS * width + 2 * tokens + text_len // ROWS * part
    return pl.pallas_call(
        functools.partial(prep_kernel, frames, share),
        out_shape=[jax.ShapeDtypeStruct((ROWS, columns), BF16)] * frames,
        name="prep",
    )(position, latents, text_kv)


def unpack(block, mine_ref, other_ref, position_scr, latents_scr, width, tokens):
    half = tokens // 2
    pieces = half // ROWS
    core = lax.rem(lax.axis_index("queue"), 2)
    for ref, place in ((mine_ref, core), (other_ref, 1 - core)):
        for piece in range(pieces):
            start = pl.multiple_of(block * tokens + place * half + piece * ROWS, ROWS)
            position_scr[pl.ds(start, ROWS), :] = ref[:, piece * width : (piece + 1) * width]
    base = pieces * width
    latents_scr[block, 0:ROWS, :] = mine_ref[:, base : base + tokens]
    latents_scr[block, ROWS : 2 * ROWS, :] = mine_ref[:, base + tokens : base + 2 * tokens]


def unpack_text(shard, mine_ref, other_ref, base, part, text_scr):
    _, text_len, padded = text_scr.shape
    core = lax.rem(lax.axis_index("queue"), 2)
    first = shard * part
    start = pl.multiple_of(lax.div(first, LANES) * LANES, LANES)
    for ref, place in ((mine_ref, core), (other_ref, 1 - core)):
        rows = jnp.concatenate(
            [
                ref[:, base + piece * part : base + (piece + 1) * part]
                for piece in range(text_len // ROWS)
            ],
            axis=0,
        ).astype(F32)
        space = -(-(part + LANES) // LANES) * LANES
        wide = jnp.concatenate([rows, jnp.zeros((text_len, space - part), F32)], axis=1)
        moved = pltpu.roll(wide, first - start, 1).astype(BF16)
        text_scr[place, :, pl.ds(start, space)] += moved


def normalize(values, scale, shift):
    center = values - jnp.mean(values, axis=-1, keepdims=True)
    variance = jnp.mean(center * center, axis=-1, keepdims=True)
    return (center * lax.rsqrt(variance + EPSILON) * scale + shift).astype(BF16)


def embed_blocks(blocks, position_scr, latents_scr, embed_ref, mods_ref, normed_scr, hidden_ref):
    tokens = latents_scr.shape[2]
    embed = jnp.concatenate([embed_ref[...], embed_ref[...]], axis=0)
    scale = 1.0 + mods_ref[1:2, :]
    shift = mods_ref[0:1, :]

    def one(block, carry):
        rows = pl.ds(pl.multiple_of(block * tokens, tokens), tokens)
        hidden = dot(latents_scr[block], embed, TN) + position_scr[rows, :].astype(F32)
        if hidden_ref is not None:
            hidden_ref[rows, :] = hidden
        normed_scr[rows, :] = normalize(hidden, scale, shift)
        return carry

    lax.fori_loop(0, blocks, one, 0, unroll=True)


def head_sums(width, head):
    column = lax.broadcasted_iota(jnp.int32, (width, LANES), 0)
    first = lax.broadcasted_iota(jnp.int32, (width, LANES), 1) * head
    return jnp.where((column >= first) & (column < first + head), 1.0, 0.0).astype(BF16)


def head_spread(width, head):
    column = lax.broadcasted_iota(jnp.int32, (LANES, width), 1)
    first = lax.broadcasted_iota(jnp.int32, (LANES, width), 0) * head
    one = jnp.where((column >= first) & (column < first + head), 1.0, 0.0).astype(BF16)
    return jnp.concatenate([one, one], axis=0)


def spread(values, spread_matrix):
    high, low = split_parts(values)
    return dot(jnp.concatenate([high, low], axis=1), spread_matrix)


def head_norm(values, gain, head, sums_matrix, spread_matrix):
    wide = values.astype(F32)
    squares = dot((wide * wide).astype(BF16), sums_matrix) * (1.0 / head)
    factor = spread(lax.rsqrt(squares + EPSILON), spread_matrix)
    return (wide * factor * gain).astype(BF16)


def project(normed_scr, weight_ref, first, last, out_ref, chunk=256):
    for start in range(first, last, chunk):
        end = min(start + chunk, last)
        out_ref[:, start - first : end - first] = dot(
            normed_scr[...], weight_ref[:, start:end]
        ).astype(BF16)


def norm_rows(source, columns, target, gain, head, sums_matrix, spread_matrix, step=128):
    def one(i, carry):
        rows = pl.ds(pl.multiple_of(i * step, step), step)
        target[rows, :] = head_norm(
            source[rows, columns], gain, head, sums_matrix, spread_matrix
        )
        return carry

    lax.fori_loop(0, target.shape[0] // step, one, 0, unroll=True)


def window(first, last, width):
    start = first // LANES * LANES
    end = min(-(-last // LANES) * LANES, width)
    return start, end


def lane_mask(shape, first, last):
    lane = lax.broadcasted_iota(jnp.int32, shape, 1)
    return (lane >= first) & (lane < last)


def keep(values, first, last):
    return jnp.where(lane_mask(values.shape, first, last), values, jnp.zeros_like(values))


def attend_self(q_ref, k_scr, v_ref, v_base, num_ref, sum_ref, head, heads, fresh, q_step):
    queries, width = q_ref.shape
    keys = k_scr.shape[0]

    def tile(i, carry):
        rows = pl.ds(pl.multiple_of(i * q_step, q_step), q_step)
        sums = jnp.zeros((q_step, LANES), F32)
        for h in range(heads):
            first, last = h * head, (h + 1) * head
            start, end = window(first, last, width)
            in_first, in_last = first - start, last - start
            q = keep(q_ref[rows, start:end], in_first, in_last)
            scores = dot(q, k_scr[:, start:end], NT)
            weights = jnp.exp2(scores).astype(BF16)
            v = keep(v_ref[:, v_base + start : v_base + end], in_first, in_last)
            mark = lane_mask((keys, LANES), h, h + 1)
            if end - start == LANES:
                ones = jnp.where(mark, 1.0, 0.0).astype(BF16)
                both = dot(weights, jnp.concatenate([v, ones], axis=1))
                sums = sums + both[:, LANES:]
                num_ref[rows, start:end] += both[:, :LANES]
            else:
                lead = jnp.where(mark, jnp.ones((), BF16), v[:, :LANES])
                both = dot(weights, jnp.concatenate([lead, v[:, LANES:]], axis=1))
                tops = lane_mask((q_step, LANES), 0, heads)
                left = both[:, :LANES]
                sums = sums + jnp.where(tops, left, 0.0)
                num_ref[rows, start : start + LANES] += jnp.where(tops, 0.0, left)
                num_ref[rows, start + LANES : end] += both[:, LANES:]
        sum_ref[rows, :] += sums
        return carry

    lax.fori_loop(0, queries // q_step, tile, 0, unroll=True)


def attend_text(q_ref, tk_scr, tv_scr, num_ref, sum_ref, head, heads, q_step):
    queries, width = q_ref.shape
    keys = tk_scr.shape[0]

    def tile(i, carry):
        rows = pl.ds(pl.multiple_of(i * q_step, q_step), q_step)
        sums = jnp.zeros((q_step, LANES), F32)
        for pair in range(0, heads, 2):
            first, middle, last = pair * head, (pair + 1) * head, (pair + 2) * head
            start, end = window(first, last, width)
            spans = ((first - start, middle - start), (middle - start, last - start))
            k = jnp.concatenate([keep(tk_scr[:, start:end], *span) for span in spans], axis=0)
            v = jnp.concatenate([keep(tv_scr[:, start:end], *span) for span in spans], axis=0)
            ones = jnp.concatenate(
                [
                    jnp.where(lane_mask((keys, LANES), h, h + 1), 1.0, 0.0).astype(BF16)
                    for h in (pair, pair + 1)
                ],
                axis=0,
            )
            weights = jnp.exp2(dot(q_ref[rows, start:end], k, NT)).astype(BF16)
            num_ref[rows, start:end] += dot(weights, v)
            sums = sums + dot(weights, ones)
        sum_ref[rows, :] = sums
        return carry

    lax.fori_loop(0, queries // q_step, tile, 0, unroll=True)


def own_kernel(
    frames, head, heads, *refs
):
    mine = refs[:frames]
    other = refs[frames : 2 * frames]
    (embed_ref, mods_ref, weight_ref, gains_ref, q_ref, hidden_ref, num_ref, sum_ref) = refs[
        2 * frames : 2 * frames + 8
    ]
    position_scr, latents_scr, normed_scr, proj_scr, k_scr = refs[2 * frames + 8 :]
    width = embed_ref.shape[1]
    tokens = latents_scr.shape[2]
    for block in range(frames):
        unpack(block, mine[block], other[block], position_scr, latents_scr, width, tokens)
    embed_blocks(
        frames, position_scr, latents_scr, embed_ref, mods_ref, normed_scr, hidden_ref
    )
    project(normed_scr, weight_ref, 0, 3 * width, proj_scr)
    sums_matrix = head_sums(width, head)
    spread_matrix = head_spread(width, head)
    norm_rows(
        proj_scr, slice(0, width), q_ref, gains_ref[0:1, :], head, sums_matrix, spread_matrix
    )
    norm_rows(
        proj_scr,
        slice(width, 2 * width),
        k_scr,
        gains_ref[1:2, :],
        head,
        sums_matrix,
        spread_matrix,
    )
    num_ref[...] = jnp.zeros_like(num_ref)
    sum_ref[...] = jnp.zeros_like(sum_ref)
    attend_self(q_ref, k_scr, proj_scr, 2 * width, num_ref, sum_ref, head, heads, True, 256)


def rest_kernel(frames, head, heads, columns, part, *refs):
    count = frames * (columns + 1)
    mine = refs[:count]
    other = refs[count : 2 * count]
    (
        embed_ref,
        mods_ref,
        weight_ref,
        gains_ref,
        q_ref,
        hidden_ref,
        num_in_ref,
        sum_in_ref,
        out_weight_ref,
        final_weight_ref,
    ) = refs[2 * count : 2 * count + 10]
    velocity_refs = refs[2 * count + 10 : 2 * count + 10 + frames]
    (
        position_scr,
        latents_scr,
        normed_scr,
        proj_scr,
        k_scr,
        num_ref,
        sum_ref,
        text_scr,
        tk_scr,
        tnum_scr,
        tsum_scr,
        attention_scr,
    ) = refs[2 * count + 10 + frames :]
    width = embed_ref.shape[1]
    tokens = latents_scr.shape[2]
    sums_matrix = head_sums(width, head)
    spread_matrix = head_spread(width, head)
    num_ref[...] = num_in_ref[...]
    sum_ref[...] = sum_in_ref[...]
    for column in range(columns):
        for block in range(frames):
            index = (column + 1) * frames + block
            unpack(block, mine[index], other[index], position_scr, latents_scr, width, tokens)
        embed_blocks(frames, position_scr, latents_scr, embed_ref, mods_ref, normed_scr, None)
        project(normed_scr, weight_ref, width, 3 * width, proj_scr)
        norm_rows(
            proj_scr,
            slice(0, width),
            k_scr,
            gains_ref[1:2, :],
            head,
            sums_matrix,
            spread_matrix,
        )
        attend_self(q_ref, k_scr, proj_scr, width, num_ref, sum_ref, head, heads, False, 256)

    text_scr[...] = jnp.zeros_like(text_scr)
    base = tokens // 2 // ROWS * width + 2 * tokens
    place = lax.axis_index("seq")
    for column in range(columns + 1):
        for block in range(frames):
            shard = jnp.bitwise_xor(place, block * (columns + 1) + column)
            index = column * frames + block
            unpack_text(shard, mine[index], other[index], base, part, text_scr)
    norm_rows(
        text_scr.at[0],
        slice(0, width),
        tk_scr,
        gains_ref[1:2, :],
        head,
        sums_matrix,
        spread_matrix,
    )
    tnum_scr[...] = jnp.zeros_like(tnum_scr)
    attend_text(q_ref, tk_scr, text_scr.at[1], tnum_scr, tsum_scr, head, heads, 256)

    def mix(i, carry):
        rows = pl.ds(pl.multiple_of(i * LANES, LANES), LANES)
        used = lane_mask((LANES, LANES), 0, heads)
        own = spread(jnp.where(used, 1.0 / sum_ref[rows, :], 0.0), spread_matrix)
        text = spread(jnp.where(used, 1.0 / tsum_scr[rows, :], 0.0), spread_matrix)
        attention_scr[rows, :] = (
            num_ref[rows, :] * own + tnum_scr[rows, :] * text
        ).astype(BF16)
        return carry

    lax.fori_loop(0, q_ref.shape[0] // LANES, mix, 0)
    num_ref[...] = dot(attention_scr[...], out_weight_ref[...])
    gate = mods_ref[2:3, :]
    shift = mods_ref[3:4, :]
    scale = 1.0 + mods_ref[4:5, :]
    for block in range(frames):
        rows = slice(block * tokens, (block + 1) * tokens)
        hidden = hidden_ref[rows, :] + gate * num_ref[rows, :]
        normed = normalize(hidden, scale, shift)
        velocity_refs[block][...] = dot(
            final_weight_ref[...], normed, (((0,), (1,)), ((), ()))
        )


def finish_kernel(
    frames,
    share,
    step_ref,
    levels_ref,
    latents_ref,
    *refs,
):
    arrived = refs[:frames]
    velocity_ref, moved_ref, first_ref = refs[frames:]
    own_frame = lax.div(lax.axis_index("seq"), share)
    for d in range(frames):
        frame = jnp.bitwise_xor(own_frame, d)
        velocity_ref[frame] = arrived[d][...]
    for frame in range(frames):
        index = step_ref[frame]
        size = levels_ref[index + 1] - levels_ref[index]
        updated = latents_ref[frame] + size * velocity_ref[frame]
        if frame == 0:
            first_ref[...] = updated
        else:
            moved_ref[frame - 1] = updated
    moved_ref[frames - 1] = jnp.zeros_like(first_ref)


def vmem(count):
    return [pl.BlockSpec(memory_space=pltpu.VMEM)] * count


def body(
    latents,
    step_index,
    levels,
    modulation,
    embed_weight,
    position,
    qkv_weight,
    q_gain,
    k_gain,
    text_kv,
    out_weight,
    final_weight,
    new_noise,
):
    frames, channels, tokens = latents.shape
    width = embed_weight.shape[1]
    head = q_gain.shape[0]
    heads = width // head
    seq = lax.axis_size("seq")
    queue = lax.axis_size("queue")
    share = seq // frames
    queries = frames * tokens
    own_frame = lax.axis_index("seq") // share

    def over_frames(value, d):
        return lax.ppermute(value, "seq", [(i, i ^ (d * share)) for i in range(seq)])

    def over_columns(value, d):
        return lax.ppermute(value, "seq", [(i, i ^ d) for i in range(seq)])

    def over_cores(value):
        return lax.ppermute(value, "queue", [(i, i ^ 1) for i in range(queue)])

    index = lax.dynamic_index_in_dim(step_index, own_frame, 0, keepdims=False)
    mods = lax.dynamic_index_in_dim(modulation, index, 0, keepdims=False)
    factor = math.log2(math.e) / math.sqrt(head)
    gains = jnp.stack([jnp.tile(q_gain * factor, heads), jnp.tile(k_gain, heads)])

    near = functools.partial(pltpu.with_memory_space_constraint, memory_space=pltpu.VMEM)
    qkv_weight, out_weight = near(qkv_weight), near(out_weight)
    sent = prep(position, latents, text_kv, frames, share)
    mine = [sent[0]] + [over_frames(sent[d], d) for d in range(1, frames)]
    other = [over_cores(value) for value in mine]
    columns = share - 1
    mine_far = [over_columns(value, d) for d in range(1, share) for value in mine]
    other_far = [over_cores(value) for value in mine_far]

    params = pltpu.CompilerParams(vmem_limit_bytes=VMEM_LIMIT)
    blocks = [
        pltpu.VMEM((queries, width), BF16),
        pltpu.VMEM((frames, 2 * channels, tokens), BF16),
        pltpu.VMEM((queries, width), BF16),
    ]
    q_hat, hidden, num, sums = pl.pallas_call(
        functools.partial(own_kernel, frames, head, heads),
        out_shape=[
            pltpu.VMEM((queries, width), BF16),
            pltpu.VMEM((queries, width), F32),
            pltpu.VMEM((queries, width), F32),
            pltpu.VMEM((queries, LANES), F32),
        ],
        in_specs=vmem(2 * frames + 4),
        out_specs=vmem(4),
        scratch_shapes=blocks
        + [pltpu.VMEM((queries, 3 * width), BF16), pltpu.VMEM((queries, width), BF16)],
        compiler_params=params,
        name="own_column",
    )(*mine, *other, embed_weight, mods, qkv_weight, gains)

    text_len = text_kv.shape[1]
    velocities = pl.pallas_call(
        functools.partial(rest_kernel, frames, head, heads, columns, text_kv.shape[2]),
        out_shape=[jax.ShapeDtypeStruct((channels, tokens), F32)] * frames,
        in_specs=vmem(2 * frames * share + 10),
        out_specs=vmem(frames),
        scratch_shapes=blocks
        + [
            pltpu.VMEM((queries, 2 * width), BF16),
            pltpu.VMEM((queries, width), BF16),
            pltpu.VMEM((queries, width), F32),
            pltpu.VMEM((queries, LANES), F32),
            pltpu.VMEM((2, text_len, width + 2 * LANES), BF16),
            pltpu.VMEM((text_len, width), BF16),
            pltpu.VMEM((queries, width), F32),
            pltpu.VMEM((queries, LANES), F32),
            pltpu.VMEM((queries, width), BF16),
        ],
        compiler_params=params,
        name="rest",
    )(
        *mine,
        *mine_far,
        *other,
        *other_far,
        embed_weight,
        mods,
        qkv_weight,
        gains,
        q_hat,
        hidden,
        num,
        sums,
        out_weight,
        final_weight,
    )

    arrived = [velocities[0]] + [over_frames(velocities[d], d) for d in range(1, frames)]
    smem = pl.BlockSpec(memory_space=pltpu.SMEM)
    velocity, moved, first = pl.pallas_call(
        functools.partial(finish_kernel, frames, share),
        out_shape=[
            jax.ShapeDtypeStruct((frames, channels, tokens), F32),
            jax.ShapeDtypeStruct((frames, channels, tokens), F32),
            jax.ShapeDtypeStruct((channels, tokens), F32),
        ],
        in_specs=[smem, smem] + vmem(frames + 1),
        out_specs=vmem(3),
        name="finish",
    )(step_index, levels, latents, *arrived)
    came = lax.ppermute(first, "queue", [(i, i - 1) for i in range(1, queue)])
    at_end = lax.axis_index("queue") == queue - 1
    came = jnp.where(at_end, new_noise, came)
    advanced = lax.dynamic_update_slice_in_dim(moved, came[None], frames - 1, 0)
    return (advanced, velocity)


def solution(mesh):
    in_specs = (
        P("queue", None, "seq"),
        P("queue"),
        P(),
        P(),
        P(),
        P("seq", None),
        P(),
        P(),
        P(),
        P(None, None, "seq"),
        P(),
        P(),
        P(None, "seq"),
    )
    out_specs = (P("queue", None, "seq"), P("queue", None, "seq"))
    return jax.shard_map(body, mesh=mesh, in_specs=in_specs, out_specs=out_specs, check_vma=False)
```

```python
import functools
import math

import jax
import jax.numpy as jnp
from jax import lax
from jax.experimental import pallas as pl
from jax.experimental.pallas import tpu as pltpu
from jax.sharding import PartitionSpec as P

EPSILON = 1e-06
LANES = 128
ROWS = 16
F32 = jnp.float32
BF16 = jnp.bfloat16
VMEM_LIMIT = 24 * 1024 * 1024
NN = (((1,), (0,)), ((), ()))
NT = (((1,), (1,)), ((), ()))
TN = (((0,), (0,)), ((), ()))


def dot(a, b, dims=NN):
    return lax.dot_general(a, b, dims, preferred_element_type=F32)


def split_parts(values):
    high = values.astype(BF16)
    low = (values - high.astype(F32)).astype(BF16)
    return high, low


class Sizes:
    def __init__(self, latents, position, text, q_gain, seq):
        self.frames, self.channels, self.tokens = latents.shape
        self.width = position.shape[1]
        self.head = q_gain.shape[0]
        self.heads = self.width // self.head
        self.seq = seq
        self.share = seq // self.frames
        self.queries = self.frames * self.tokens
        _, self.part, self.text_len = text.shape
        self.half = self.tokens // 2
        self.pieces = self.half // ROWS
        self.text_pieces = -(-self.part // ROWS)
        self.latents_at = self.pieces * self.width
        self.text_at = self.latents_at + 2 * self.frames * self.tokens
        self.payload = self.text_at + self.text_pieces * self.text_len


def prep_kernel(sizes, position_ref, latents_ref, text_ref, payload_ref):
    core = lax.rem(lax.axis_index("queue"), 2)
    width, tokens = sizes.width, sizes.tokens
    for piece in range(sizes.pieces):
        start = pl.multiple_of(core * sizes.half + piece * ROWS, ROWS)
        payload_ref[:, piece * width : (piece + 1) * width] = position_ref[pl.ds(start, ROWS), :]
    for frame in range(sizes.frames):
        high, low = split_parts(latents_ref[frame])
        at = sizes.latents_at + 2 * frame * tokens
        payload_ref[:, at : at + tokens] = high
        payload_ref[:, at + tokens : at + 2 * tokens] = low
    for piece in range(sizes.text_pieces):
        first, last = piece * ROWS, min((piece + 1) * ROWS, sizes.part)
        rows = text_ref[core, first:last, :]
        if last - first < ROWS:
            blank = jnp.zeros((ROWS - (last - first), sizes.text_len), BF16)
            rows = jnp.concatenate([rows, blank], axis=0)
        at = sizes.text_at + piece * sizes.text_len
        payload_ref[:, at : at + sizes.text_len] = rows


def unpack(sizes, block, mine_ref, other_ref, position_scr, latents_scr):
    width, tokens = sizes.width, sizes.tokens
    core = lax.rem(lax.axis_index("queue"), 2)
    frame = lax.rem(lax.axis_index("seq"), sizes.frames)
    for ref, place in ((mine_ref, core), (other_ref, 1 - core)):
        for piece in range(sizes.pieces):
            start = pl.multiple_of(block * tokens + place * sizes.half + piece * ROWS, ROWS)
            position_scr[pl.ds(start, ROWS), :] = ref[:, piece * width : (piece + 1) * width]
    at = pl.multiple_of(sizes.latents_at + 2 * frame * tokens, LANES)
    both = mine_ref[:, pl.ds(at, 2 * tokens)]
    latents_scr[block, 0:ROWS, :] = both[:, :tokens]
    latents_scr[block, ROWS : 2 * ROWS, :] = both[:, tokens:]


def unpack_text(sizes, shard, mine_ref, other_ref, text_scr):
    core = lax.rem(lax.axis_index("queue"), 2)
    for ref, place in ((mine_ref, core), (other_ref, 1 - core)):
        for piece in range(sizes.text_pieces):
            first, last = piece * ROWS, min((piece + 1) * ROWS, sizes.part)
            at = sizes.text_at + piece * sizes.text_len
            rows = ref[:, at : at + sizes.text_len].astype(F32)
            start = pl.multiple_of(shard * sizes.part + first, 8)
            text_scr[place, pl.ds(start, last - first), :] = rows[: last - first]


def normalize(values, scale, shift):
    center = values - jnp.mean(values, axis=-1, keepdims=True)
    variance = jnp.mean(center * center, axis=-1, keepdims=True)
    return (center * lax.rsqrt(variance + EPSILON) * scale + shift).astype(BF16)


def embed_blocks(sizes, blocks, position_scr, latents_scr, embed_ref, rows_ref, normed_scr, hidden):
    tokens = sizes.tokens
    embed = jnp.concatenate([embed_ref[...], embed_ref[...]], axis=0)
    for block in range(blocks):
        rows = slice(block * tokens, (block + 1) * tokens)
        values = dot(latents_scr[block], embed, TN) + position_scr[rows, :].astype(F32)
        if hidden is not None:
            hidden[rows, :] = values
        normed_scr[rows, :] = normalize(values, rows_ref[1:2, :], rows_ref[0:1, :])


def head_sums(sizes):
    column = lax.broadcasted_iota(jnp.int32, (sizes.width, LANES), 0)
    first = lax.broadcasted_iota(jnp.int32, (sizes.width, LANES), 1) * sizes.head
    inside = (column >= first) & (column < first + sizes.head)
    return jnp.where(inside, 1.0, 0.0).astype(BF16)


def head_spread(sizes):
    column = lax.broadcasted_iota(jnp.int32, (LANES, sizes.width), 1)
    first = lax.broadcasted_iota(jnp.int32, (LANES, sizes.width), 0) * sizes.head
    inside = (column >= first) & (column < first + sizes.head)
    one = jnp.where(inside, 1.0, 0.0).astype(BF16)
    return jnp.concatenate([one, one], axis=0)


def spread(values, spread_matrix):
    high, low = split_parts(values)
    return dot(jnp.concatenate([high, low], axis=1), spread_matrix)


def norm_rows(sizes, source, target, gain, sums_matrix, spread_matrix, step=128):
    for start in range(0, source.shape[0], step):
        wide = source[start : start + step, :].astype(F32)
        squares = dot((wide * wide).astype(BF16), sums_matrix) * (1.0 / sizes.head)
        factor = spread(lax.rsqrt(squares + EPSILON), spread_matrix)
        target[start : start + step, :] = (wide * factor * gain).astype(BF16)


def project(normed_scr, weight_ref, first, last, out_ref, chunk=256):
    for start in range(first, last, chunk):
        end = min(start + chunk, last)
        out_ref[:, start - first : end - first] = dot(
            normed_scr[...], weight_ref[:, start:end]
        ).astype(BF16)


def window(first, last, width):
    start = first // LANES * LANES
    end = min(-(-last // LANES) * LANES, width)
    return start, end


def lane_mask(shape, first, last, axis=1):
    lane = lax.broadcasted_iota(jnp.int32, shape, axis)
    return (lane >= first) & (lane < last)


def keep(values, first, last, axis=1):
    inside = lane_mask(values.shape, first, last, axis)
    return jnp.where(inside, values, jnp.zeros_like(values))


def attend_self(sizes, q_ref, k_ref, v_ref, num_ref, sum_ref, fresh, q_step=256):
    queries, width = q_ref.shape
    keys = k_ref.shape[0]
    for q_start in range(0, queries, q_step):
        rows = slice(q_start, q_start + q_step)
        sums = jnp.zeros((q_step, LANES), F32)
        pending = jnp.zeros((q_step, LANES), F32)
        for h in range(sizes.heads):
            first, last = h * sizes.head, (h + 1) * sizes.head
            start, end = window(first, last, width)
            span = (first - start, last - start)
            scores = dot(keep(q_ref[rows, start:end], *span), k_ref[:, start:end], NT)
            weights = jnp.exp2(scores).astype(BF16)
            v = keep(v_ref[:, start:end], *span)
            mark = lane_mask((keys, LANES), h, h + 1)
            if end - start == LANES:
                ones = jnp.where(mark, 1.0, 0.0).astype(BF16)
                both = dot(weights, jnp.concatenate([v, ones], axis=1))
                sums = sums + both[:, LANES:]
                pending = pending + both[:, :LANES]
            else:
                lead = jnp.where(mark, jnp.ones((), BF16), v[:, :LANES])
                both = dot(weights, jnp.concatenate([lead, v[:, LANES:]], axis=1))
                tops = lane_mask((q_step, LANES), 0, sizes.heads)
                left = both[:, :LANES]
                sums = sums + jnp.where(tops, left, 0.0)
                pending = pending + jnp.where(tops, 0.0, left)
            if last >= start + LANES:
                if fresh:
                    num_ref[rows, start : start + LANES] = pending
                else:
                    num_ref[rows, start : start + LANES] += pending
                wide = end - start > LANES
                pending = both[:, LANES:] if wide else jnp.zeros((q_step, LANES), F32)
        if fresh:
            sum_ref[rows, :] = sums
        else:
            sum_ref[rows, :] += sums


def attend_text(sizes, q_ref, k_scr, v_scr, num_ref, sum_ref, q_step=256):
    queries, width = q_ref.shape
    keys = k_scr.shape[1]
    for q_start in range(0, queries, q_step):
        rows = slice(q_start, q_start + q_step)
        sums = jnp.zeros((q_step, LANES), F32)
        for pair in range(0, sizes.heads, 2):
            edges = [(pair + i) * sizes.head for i in range(3)]
            start, end = window(edges[0], edges[2], width)
            spans = [(edges[i] - start, edges[i + 1] - start) for i in range(2)]
            k = jnp.concatenate([keep(k_scr[start:end, :], *span, 0) for span in spans], axis=1)
            v = jnp.concatenate([keep(v_scr[start:end, :], *span, 0) for span in spans], axis=1)
            ones = [
                jnp.where(lane_mask((keys, LANES), h, h + 1), 1.0, 0.0).astype(BF16)
                for h in (pair, pair + 1)
            ]
            weights = jnp.exp2(dot(q_ref[rows, start:end], k)).astype(BF16)
            num_ref[rows, start:end] += dot(weights, v, NT)
            sums = sums + dot(weights, jnp.concatenate(ones, axis=0))
        sum_ref[rows, :] = sums


def first_kernel(
    sizes, step_ref, modulation_ref, q_gain_ref, k_gain_ref, mine, other, embed_ref, weight_ref,
    rows_ref, q_ref, k_ref, v_ref, hidden_ref, position_scr, latents_scr, normed_scr, proj_scr,
):
    width = sizes.width
    frame = lax.rem(lax.axis_index("seq"), sizes.frames)
    index = step_ref[frame]
    for i in range(5):
        row = modulation_ref[i, pl.ds(index, 1), :]
        rows_ref[i : i + 1, :] = row + 1.0 if i in (1, 4) else row
    factor = math.log2(math.e) / math.sqrt(sizes.head)
    for h in range(sizes.heads):
        rows_ref[5:6, h * sizes.head : (h + 1) * sizes.head] = q_gain_ref[...] * factor
        rows_ref[6:7, h * sizes.head : (h + 1) * sizes.head] = k_gain_ref[...]
    rows_ref[7:8, :] = jnp.zeros((1, width), F32)
    unpack(sizes, 0, mine, other, position_scr, latents_scr)
    embed_blocks(
        sizes, 1, position_scr, latents_scr, embed_ref, rows_ref, normed_scr, hidden_ref
    )
    project(normed_scr, weight_ref, 0, 2 * width, proj_scr)
    project(normed_scr, weight_ref, 2 * width, 3 * width, v_ref)
    matrices = head_sums(sizes), head_spread(sizes)
    norm_rows(sizes, proj_scr.at[:, :width], q_ref, rows_ref[5:6, :], *matrices)
    norm_rows(sizes, proj_scr.at[:, width:], k_ref, rows_ref[6:7, :], *matrices)


def own_kernel(sizes, *refs):
    count = sizes.frames - 1
    mine, other = refs[:count], refs[count : 2 * count]
    (
        embed_ref, rows_ref, weight_ref, q_one, k_one, v_one, hidden_one,
        q_ref, k_ref, v_ref, hidden_ref, position_scr, latents_scr, normed_scr, proj_scr,
    ) = refs[2 * count :]
    width, tokens = sizes.width, sizes.tokens
    for block in range(count):
        unpack(sizes, block, mine[block], other[block], position_scr, latents_scr)
    q_ref[:tokens, :] = q_one[...]
    k_ref[:tokens, :] = k_one[...]
    v_ref[:tokens, :] = v_one[...]
    hidden_ref[:tokens, :] = hidden_one[...]
    embed_blocks(
        sizes, count, position_scr, latents_scr, embed_ref, rows_ref, normed_scr,
        hidden_ref.at[tokens:, :],
    )
    project(normed_scr, weight_ref, 0, 2 * width, proj_scr)
    project(normed_scr, weight_ref, 2 * width, 3 * width, v_ref.at[tokens:, :])
    matrices = head_sums(sizes), head_spread(sizes)
    norm_rows(
        sizes, proj_scr.at[:, :width], q_ref.at[tokens:, :], rows_ref[5:6, :], *matrices
    )
    norm_rows(
        sizes, proj_scr.at[:, width:], k_ref.at[tokens:, :], rows_ref[6:7, :], *matrices
    )


def attend_kernel(sizes, q_ref, k_ref, v_ref, num_ref, sum_ref):
    attend_self(sizes, q_ref, k_ref, v_ref, num_ref, sum_ref, True)


def rest_kernel(sizes, *refs):
    frames, share, width, tokens = sizes.frames, sizes.share, sizes.width, sizes.tokens
    count = frames * share
    mine, other = refs[:count], refs[count : 2 * count]
    (
        embed_ref, rows_ref, weight_ref, q_ref, hidden_ref, num_in_ref, sum_in_ref,
        out_weight_ref, final_weight_ref,
    ) = refs[2 * count : 2 * count + 9]
    velocity_refs = refs[2 * count + 9 : 2 * count + 9 + frames]
    (
        position_scr, latents_scr, normed_scr, proj_scr, k_scr, v_scr, num_ref, sum_ref,
        text_scr, tk_scr, tv_scr, tnum_scr, tsum_scr, attention_scr,
    ) = refs[2 * count + 9 + frames :]
    sums_matrix, spread_matrix = head_sums(sizes), head_spread(sizes)
    num_ref[...] = num_in_ref[...]
    sum_ref[...] = sum_in_ref[...]
    for group in range(1, share):
        for block in range(frames):
            at = group * frames + block
            unpack(sizes, block, mine[at], other[at], position_scr, latents_scr)
        embed_blocks(
            sizes, frames, position_scr, latents_scr, embed_ref, rows_ref, normed_scr, None
        )
        project(normed_scr, weight_ref, width, 2 * width, proj_scr)
        project(normed_scr, weight_ref, 2 * width, 3 * width, v_scr)
        norm_rows(sizes, proj_scr, k_scr, rows_ref[6:7, :], sums_matrix, spread_matrix)
        attend_self(sizes, q_ref, k_scr, v_scr, num_ref, sum_ref, False)

    place = lax.axis_index("seq")
    for at in range(count):
        unpack_text(sizes, jnp.bitwise_xor(place, at), mine[at], other[at], text_scr)
    gain_column = jnp.transpose(jnp.broadcast_to(rows_ref[6:7, :], (LANES, width)))[:, 0:1]
    for h in range(sizes.heads):
        rows = slice(h * sizes.head, (h + 1) * sizes.head)
        values = text_scr[0, rows, :]
        mean = jnp.mean(values * values, axis=0, keepdims=True)
        text_scr[0, rows, :] = values * lax.rsqrt(mean + EPSILON) * gain_column[rows]
    tk_scr[...] = text_scr[0].astype(BF16)
    tv_scr[...] = text_scr[1].astype(BF16)
    tnum_scr[...] = jnp.zeros_like(tnum_scr)
    attend_text(sizes, q_ref, tk_scr, tv_scr, tnum_scr, tsum_scr)

    for start in range(0, sizes.queries, LANES):
        rows = slice(start, start + LANES)
        used = lane_mask((LANES, LANES), 0, sizes.heads)
        own = spread(jnp.where(used, 1.0 / sum_ref[rows, :], 0.0), spread_matrix)
        text = spread(jnp.where(used, 1.0 / tsum_scr[rows, :], 0.0), spread_matrix)
        attention_scr[rows, :] = (num_ref[rows, :] * own + tnum_scr[rows, :] * text).astype(BF16)
    num_ref[...] = dot(attention_scr[...], out_weight_ref[...])
    for block in range(frames):
        rows = slice(block * tokens, (block + 1) * tokens)
        hidden = hidden_ref[rows, :] + rows_ref[2:3, :] * num_ref[rows, :]
        normed = normalize(hidden, rows_ref[4:5, :], rows_ref[3:4, :])
        velocity_refs[block][...] = dot(final_weight_ref[...], normed, NT)


def finish_kernel(sizes, step_ref, levels_ref, latents_ref, *refs):
    frames = sizes.frames
    arrived = refs[:frames]
    velocity_ref, moved_ref, first_ref = refs[frames:]
    own_frame = lax.rem(lax.axis_index("seq"), frames)
    for d in range(frames):
        velocity_ref[jnp.bitwise_xor(own_frame, d)] = arrived[d][...]
    for frame in range(frames):
        index = step_ref[frame]
        size = levels_ref[index + 1] - levels_ref[index]
        updated = latents_ref[frame] + size * velocity_ref[frame]
        if frame == 0:
            first_ref[...] = updated
        else:
            moved_ref[frame - 1] = updated
    moved_ref[frames - 1] = jnp.zeros_like(first_ref)


def kernel(function, sizes, name, ins, outs, scratch, us, smem=0):
    spec = pl.BlockSpec(memory_space=pltpu.VMEM)
    scalars = pl.BlockSpec(memory_space=pltpu.SMEM)
    return pl.pallas_call(
        functools.partial(function, sizes),
        out_shape=outs,
        in_specs=[scalars] * smem + [spec] * (ins - smem),
        out_specs=jax.tree.map(lambda _: spec, outs),
        scratch_shapes=scratch,
        compiler_params=pltpu.CompilerParams(vmem_limit_bytes=VMEM_LIMIT),
        cost_estimate=pl.CostEstimate(
            flops=int(us * 1e9), bytes_accessed=int(us * 1e6), transcendentals=0
        ),
        name=name,
    )


def body(
    latents,
    step_index,
    levels,
    modulation,
    embed_weight,
    position,
    qkv_weight,
    q_gain,
    k_gain,
    text_kv,
    out_weight,
    final_weight,
    new_noise,
):
    text = jnp.swapaxes(text_kv, 1, 2)
    modulation = jnp.swapaxes(modulation, 0, 1)
    sizes = Sizes(latents, position, text, q_gain, lax.axis_size("seq"))
    frames, width, tokens, queries = sizes.frames, sizes.width, sizes.tokens, sizes.queries
    queue = lax.axis_size("queue")

    def swapped(value, d):
        return lax.ppermute(value, "seq", [(i, i ^ d) for i in range(sizes.seq)])

    def over_cores(value):
        return lax.ppermute(value, "queue", [(i, i ^ 1) for i in range(queue)])

    near = functools.partial(pltpu.with_memory_space_constraint, memory_space=pltpu.VMEM)
    qkv_weight, out_weight = near(qkv_weight), near(out_weight)

    payload = kernel(
        prep_kernel, sizes, "prep", 3, pltpu.VMEM((ROWS, sizes.payload), BF16), [], 1.5
    )(position, latents, text)
    mine = [payload] + [swapped(payload, d) for d in range(1, frames)]
    for group in range(1, sizes.share):
        far = swapped(payload, group * frames)
        mine += [far] + [swapped(far, d) for d in range(1, frames)]
    other = [over_cores(value) for value in mine]

    def blocks(count):
        return [
            pltpu.VMEM((count * tokens, width), BF16),
            pltpu.VMEM((count, 2 * ROWS, tokens), BF16),
            pltpu.VMEM((count * tokens, width), BF16),
        ]

    def token_arrays(count):
        rows = count * tokens
        return [pltpu.VMEM((rows, width), BF16)] * 3 + [pltpu.VMEM((rows, width), F32)]

    rows, *one = kernel(
        first_kernel,
        sizes,
        "first",
        8,
        [pltpu.VMEM((8, width), F32)] + token_arrays(1),
        blocks(1) + [pltpu.VMEM((tokens, 2 * width), BF16)],
        4,
        smem=1,
    )(
        step_index,
        modulation,
        q_gain[None],
        k_gain[None],
        mine[0],
        other[0],
        embed_weight,
        qkv_weight,
    )
    q_hat, k_hat, value, hidden = kernel(
        own_kernel,
        sizes,
        "own",
        2 * (frames - 1) + 7,
        token_arrays(frames),
        blocks(frames - 1) + [pltpu.VMEM(((frames - 1) * tokens, 2 * width), BF16)],
        8,
    )(*mine[1:frames], *other[1:frames], embed_weight, rows, qkv_weight, *one)
    sums_shape = pltpu.VMEM((queries, LANES), F32)
    num, sums = kernel(
        attend_kernel,
        sizes,
        "attend",
        3,
        [pltpu.VMEM((queries, width), F32), sums_shape],
        [],
        5,
    )(q_hat, k_hat, value)
    velocities = kernel(
        rest_kernel,
        sizes,
        "rest",
        2 * sizes.seq + 9,
        [pltpu.VMEM((sizes.channels, tokens), F32)] * frames,
        blocks(frames)
        + [pltpu.VMEM((queries, width), BF16)] * 3
        + [
            pltpu.VMEM((queries, width), F32),
            sums_shape,
            pltpu.VMEM((2, width, sizes.text_len), F32),
            pltpu.VMEM((width, sizes.text_len), BF16),
            pltpu.VMEM((width, sizes.text_len), BF16),
            pltpu.VMEM((queries, width), F32),
            sums_shape,
            pltpu.VMEM((queries, width), BF16),
        ],
        18,
    )(
        *mine,
        *other,
        embed_weight,
        rows,
        qkv_weight,
        q_hat,
        hidden,
        num,
        sums,
        out_weight,
        final_weight.T,
    )

    arrived = [velocities[0]] + [swapped(velocities[d], d) for d in range(1, frames)]
    whole = jax.ShapeDtypeStruct(latents.shape, F32)
    velocity, moved, first = kernel(
        finish_kernel,
        sizes,
        "finish",
        3 + frames,
        [whole, whole, pltpu.VMEM(latents.shape[1:], F32)],
        [],
        1,
        smem=2,
    )(step_index, levels, latents, *arrived)
    came = lax.ppermute(first, "queue", [(i, i - 1) for i in range(1, queue)])
    at_end = lax.axis_index("queue") == queue - 1
    came = jnp.where(at_end, new_noise, came)
    advanced = lax.dynamic_update_slice_in_dim(moved, came[None], frames - 1, 0)
    return (advanced, velocity)


def solution(mesh):
    in_specs = (
        P("queue", None, "seq"),
        P("queue"),
        P(),
        P(),
        P(),
        P("seq", None),
        P(),
        P(),
        P(),
        P(None, None, "seq"),
        P(),
        P(),
        P(None, "seq"),
    )
    out_specs = (P("queue", None, "seq"), P("queue", None, "seq"))
    return jax.shard_map(body, mesh=mesh, in_specs=in_specs, out_specs=out_specs, check_vma=False)
```

```python
import functools
import math

import jax
import jax.numpy as jnp
from jax import lax
from jax.experimental import pallas as pl
from jax.experimental.pallas import tpu as pltpu
from jax.sharding import PartitionSpec as P

EPSILON = 1e-06
LANES = 128
ROWS = 16
F32 = jnp.float32
BF16 = jnp.bfloat16
VMEM_LIMIT = 24 * 1024 * 1024
NN = (((1,), (0,)), ((), ()))
NT = (((1,), (1,)), ((), ()))
TN = (((0,), (0,)), ((), ()))


def dot(a, b, dims=NN):
    return lax.dot_general(a, b, dims, preferred_element_type=F32)


def split_parts(values):
    high = values.astype(BF16)
    low = (values - high.astype(F32)).astype(BF16)
    return high, low


class Sizes:
    def __init__(self, latents, position, text, q_gain, seq):
        self.frames, self.channels, self.tokens = latents.shape
        self.width = position.shape[1]
        self.head = q_gain.shape[0]
        self.heads = self.width // self.head
        self.seq = seq
        self.share = seq // self.frames
        self.queries = self.frames * self.tokens
        _, self.part, self.text_len = text.shape
        self.half = self.tokens // 2
        self.pieces = self.half // ROWS
        self.text_pieces = -(-self.part // ROWS)
        self.latents_at = self.pieces * self.width
        self.text_at = self.latents_at + 2 * self.frames * self.tokens
        self.payload = self.text_at + self.text_pieces * self.text_len


def prep_kernel(
    sizes, position_ref, latents_ref, text_ref, payload_ref, latents_scr, text_scr, sems
):
    core = lax.rem(lax.axis_index("queue"), 2)
    width, tokens = sizes.width, sizes.tokens
    copies = [
        pltpu.make_async_copy(latents_ref, latents_scr, sems.at[0]),
        pltpu.make_async_copy(text_ref.at[core], text_scr, sems.at[1]),
    ]
    for piece in range(sizes.pieces):
        start = pl.multiple_of(core * sizes.half + piece * ROWS, ROWS)
        copies.append(
            pltpu.make_async_copy(
                position_ref.at[pl.ds(start, ROWS), :],
                payload_ref.at[:, piece * width : (piece + 1) * width],
                sems.at[2 + piece],
            )
        )
    for copy in copies:
        copy.start()
    copies[0].wait()
    for frame in range(sizes.frames):
        high, low = split_parts(latents_scr[frame])
        at = sizes.latents_at + 2 * frame * tokens
        payload_ref[:, at : at + tokens] = high
        payload_ref[:, at + tokens : at + 2 * tokens] = low
    copies[1].wait()
    for piece in range(sizes.text_pieces):
        first, last = piece * ROWS, min((piece + 1) * ROWS, sizes.part)
        rows = text_scr[first:last, :]
        if last - first < ROWS:
            blank = jnp.zeros((ROWS - (last - first), sizes.text_len), BF16)
            rows = jnp.concatenate([rows, blank], axis=0)
        at = sizes.text_at + piece * sizes.text_len
        payload_ref[:, at : at + sizes.text_len] = rows
    for copy in copies[2:]:
        copy.wait()


def unpack(sizes, block, mine_ref, other_ref, position_scr, latents_scr):
    width, tokens = sizes.width, sizes.tokens
    core = lax.rem(lax.axis_index("queue"), 2)
    frame = lax.rem(lax.axis_index("seq"), sizes.frames)
    for ref, place in ((mine_ref, core), (other_ref, 1 - core)):
        for piece in range(sizes.pieces):
            start = pl.multiple_of(block * tokens + place * sizes.half + piece * ROWS, ROWS)
            position_scr[pl.ds(start, ROWS), :] = ref[:, piece * width : (piece + 1) * width]
    at = pl.multiple_of(sizes.latents_at + 2 * frame * tokens, LANES)
    both = mine_ref[:, pl.ds(at, 2 * tokens)]
    lanes = slice(block * tokens, (block + 1) * tokens)
    latents_scr[0:ROWS, lanes] = both[:, :tokens]
    latents_scr[ROWS : 2 * ROWS, lanes] = both[:, tokens:]


def own_latents(sizes, mine_ref):
    frame = lax.rem(lax.axis_index("seq"), sizes.frames)
    at = pl.multiple_of(sizes.latents_at + 2 * frame * sizes.tokens, LANES)
    both = mine_ref[:, pl.ds(at, 2 * sizes.tokens)].astype(F32)
    return both[:, : sizes.tokens] + both[:, sizes.tokens :]


def unpack_text(sizes, shard, mine_ref, other_ref, text_scr):
    core = lax.rem(lax.axis_index("queue"), 2)
    for ref, place in ((mine_ref, core), (other_ref, 1 - core)):
        for piece in range(sizes.text_pieces):
            first, last = piece * ROWS, min((piece + 1) * ROWS, sizes.part)
            at = sizes.text_at + piece * sizes.text_len
            rows = ref[:, at : at + sizes.text_len].astype(F32)
            start = pl.multiple_of(shard * sizes.part + first, 8)
            text_scr[place, pl.ds(start, last - first), :] = rows[: last - first]


def normalize(values, scale, shift):
    center = values - jnp.mean(values, axis=-1, keepdims=True)
    variance = jnp.mean(center * center, axis=-1, keepdims=True)
    return (center * lax.rsqrt(variance + EPSILON) * scale + shift).astype(BF16)


def embed_blocks(sizes, blocks, position_scr, latents_scr, embed_ref, rows_ref, normed_scr, hidden):
    tokens = sizes.tokens
    embed = jnp.concatenate([embed_ref[...], embed_ref[...]], axis=0)
    embedded = dot(latents_scr[...], embed, TN)
    for block in range(blocks):
        rows = slice(block * tokens, (block + 1) * tokens)
        values = embedded[rows] + position_scr[rows, :].astype(F32)
        if hidden is not None:
            hidden[rows, :] = values
        normed_scr[rows, :] = normalize(values, rows_ref[1:2, :], rows_ref[0:1, :])


def head_sums(sizes):
    column = lax.broadcasted_iota(jnp.int32, (sizes.width, LANES), 0)
    first = lax.broadcasted_iota(jnp.int32, (sizes.width, LANES), 1) * sizes.head
    inside = (column >= first) & (column < first + sizes.head)
    return jnp.where(inside, 1.0, 0.0).astype(BF16)


def head_spread(sizes):
    column = lax.broadcasted_iota(jnp.int32, (LANES, sizes.width), 1)
    first = lax.broadcasted_iota(jnp.int32, (LANES, sizes.width), 0) * sizes.head
    inside = (column >= first) & (column < first + sizes.head)
    one = jnp.where(inside, 1.0, 0.0).astype(BF16)
    return jnp.concatenate([one, one], axis=0)


def spread(values, spread_matrix):
    high, low = split_parts(values)
    return dot(jnp.concatenate([high, low], axis=1), spread_matrix)


def norm_rows(sizes, source, target, gain, sums_matrix, spread_matrix, step=256):
    for start in range(0, source.shape[0], step):
        wide = source[start : start + step, :].astype(F32)
        squares = dot((wide * wide).astype(BF16), sums_matrix) * (1.0 / sizes.head)
        factor = spread(lax.rsqrt(squares + EPSILON), spread_matrix)
        target[start : start + step, :] = (wide * factor * gain).astype(BF16)


def project(normed_scr, weight_ref, first, last, out_ref, chunk=256):
    for start in range(first, last, chunk):
        end = min(start + chunk, last)
        out_ref[:, start - first : end - first] = dot(
            normed_scr[...], weight_ref[:, start:end]
        ).astype(BF16)


def window(first, last, width):
    start = first // LANES * LANES
    end = min(-(-last // LANES) * LANES, width)
    return start, end


def lane_mask(shape, first, last, axis=1):
    lane = lax.broadcasted_iota(jnp.int32, shape, axis)
    return (lane >= first) & (lane < last)


def keep(values, first, last, axis=1):
    inside = lane_mask(values.shape, first, last, axis)
    return jnp.where(inside, values, jnp.zeros_like(values))


def attend_self(sizes, q_ref, k_ref, v_ref, num_ref, sum_ref, fresh, q_step=512):
    queries, width = q_ref.shape
    keys = k_ref.shape[0]
    for q_start in range(0, queries, q_step):
        rows = slice(q_start, q_start + q_step)
        sums = jnp.zeros((q_step, LANES), F32)
        pending = jnp.zeros((q_step, LANES), F32)
        for h in range(sizes.heads):
            first, last = h * sizes.head, (h + 1) * sizes.head
            start, end = window(first, last, width)
            span = (first - start, last - start)
            scores = dot(keep(q_ref[rows, start:end], *span), k_ref[:, start:end], NT)
            weights = jnp.exp2(scores).astype(BF16)
            v = keep(v_ref[:, start:end], *span)
            mark = lane_mask((keys, LANES), h, h + 1)
            if end - start == LANES:
                ones = jnp.where(mark, 1.0, 0.0).astype(BF16)
                both = dot(weights, jnp.concatenate([v, ones], axis=1))
                sums = sums + both[:, LANES:]
                pending = pending + both[:, :LANES]
            else:
                lead = jnp.where(mark, jnp.ones((), BF16), v[:, :LANES])
                both = dot(weights, jnp.concatenate([lead, v[:, LANES:]], axis=1))
                tops = lane_mask((q_step, LANES), 0, sizes.heads)
                left = both[:, :LANES]
                sums = sums + jnp.where(tops, left, 0.0)
                pending = pending + jnp.where(tops, 0.0, left)
            if last >= start + LANES:
                if fresh:
                    num_ref[rows, start : start + LANES] = pending
                else:
                    num_ref[rows, start : start + LANES] += pending
                wide = end - start > LANES
                pending = both[:, LANES:] if wide else jnp.zeros((q_step, LANES), F32)
        if fresh:
            sum_ref[rows, :] = sums
        else:
            sum_ref[rows, :] += sums


def attend_text(sizes, q_ref, k_scr, v_scr, num_ref, sum_ref, q_step=512):
    queries, width = q_ref.shape
    keys = k_scr.shape[1]
    for q_start in range(0, queries, q_step):
        rows = slice(q_start, q_start + q_step)
        sums = jnp.zeros((q_step, LANES), F32)
        pending, pending_at = None, None
        for pair in range(0, sizes.heads, 2):
            edges = [(pair + i) * sizes.head for i in range(3)]
            start, end = window(edges[0], edges[2], width)
            spans = [(edges[i] - start, edges[i + 1] - start) for i in range(2)]
            k = jnp.concatenate([keep(k_scr[start:end, :], *span, 0) for span in spans], axis=1)
            v = jnp.concatenate([keep(v_scr[start:end, :], *span, 0) for span in spans], axis=1)
            ones = [
                jnp.where(lane_mask((keys, LANES), h, h + 1), 1.0, 0.0).astype(BF16)
                for h in (pair, pair + 1)
            ]
            weights = jnp.exp2(dot(q_ref[rows, start:end], k)).astype(BF16)
            both = dot(weights, v, NT)
            sums = sums + dot(weights, jnp.concatenate(ones, axis=0))
            for at in range(start, end, LANES):
                part = both[:, at - start : at - start + LANES]
                if pending_at == at:
                    part = pending + part
                elif pending_at is not None and pending_at < at:
                    num_ref[rows, pending_at : pending_at + LANES] = pending
                pending, pending_at = part, at
        num_ref[rows, pending_at : pending_at + LANES] = pending
        sum_ref[rows, :] = sums


def first_kernel(
    sizes, step_ref, levels_ref, modulation_ref, q_gain_ref, k_gain_ref, mine, other, embed_ref, weight_ref,
    rows_ref, near_ref, q_ref, k_ref, v_ref, hidden_ref,
    position_scr, latents_scr, normed_scr, proj_scr, sems,
):
    width = sizes.width
    copies = []
    for i in range(3):
        columns = slice(i * width, (i + 1) * width)
        copies.append(
            pltpu.make_async_copy(
                weight_ref.at[:, columns], near_ref.at[:, columns], sems.at[i]
            )
        )
        copies[i].start()
    frame = lax.rem(lax.axis_index("seq"), sizes.frames)
    index = step_ref[frame]
    for i in range(5):
        row = modulation_ref[i, pl.ds(index, 1), :]
        rows_ref[i : i + 1, :] = row + 1.0 if i in (1, 4) else row
    factor = math.log2(math.e) / math.sqrt(sizes.head)
    for h in range(sizes.heads):
        rows_ref[5:6, h * sizes.head : (h + 1) * sizes.head] = q_gain_ref[...] * factor
        rows_ref[6:7, h * sizes.head : (h + 1) * sizes.head] = k_gain_ref[...]
    rows_ref[7:8, :] = jnp.full((1, width), levels_ref[index + 1] - levels_ref[index])
    unpack(sizes, 0, mine, other, position_scr, latents_scr)
    embed_blocks(
        sizes, 1, position_scr, latents_scr, embed_ref, rows_ref, normed_scr, hidden_ref
    )
    matrices = head_sums(sizes), head_spread(sizes)
    copies[0].wait()
    project(normed_scr, near_ref, 0, width, proj_scr)
    norm_rows(sizes, proj_scr, q_ref, rows_ref[5:6, :], *matrices)
    copies[1].wait()
    project(normed_scr, near_ref, width, 2 * width, proj_scr)
    norm_rows(sizes, proj_scr, k_ref, rows_ref[6:7, :], *matrices)
    copies[2].wait()
    project(normed_scr, near_ref, 2 * width, 3 * width, v_ref)


def own_kernel(sizes, *refs):
    count = sizes.frames - 1
    mine, other = refs[:count], refs[count : 2 * count]
    (
        embed_ref, rows_ref, weight_ref, q_one, k_one, v_one, hidden_one,
        q_ref, k_ref, v_ref, hidden_ref, position_scr, latents_scr, normed_scr, proj_scr,
    ) = refs[2 * count :]
    width, tokens = sizes.width, sizes.tokens
    for block in range(count):
        unpack(sizes, block, mine[block], other[block], position_scr, latents_scr)
    q_ref[:tokens, :] = q_one[...]
    k_ref[:tokens, :] = k_one[...]
    v_ref[:tokens, :] = v_one[...]
    hidden_ref[:tokens, :] = hidden_one[...]
    embed_blocks(
        sizes, count, position_scr, latents_scr, embed_ref, rows_ref, normed_scr,
        hidden_ref.at[tokens:, :],
    )
    project(normed_scr, weight_ref, 0, 2 * width, proj_scr)
    project(normed_scr, weight_ref, 2 * width, 3 * width, v_ref.at[tokens:, :])
    matrices = head_sums(sizes), head_spread(sizes)
    norm_rows(
        sizes, proj_scr.at[:, :width], q_ref.at[tokens:, :], rows_ref[5:6, :], *matrices
    )
    norm_rows(
        sizes, proj_scr.at[:, width:], k_ref.at[tokens:, :], rows_ref[6:7, :], *matrices
    )


def attend_kernel(
    sizes, q_ref, k_ref, v_ref, out_weight_ref, num_ref, sum_ref, near_ref, sem
):
    copy = pltpu.make_async_copy(out_weight_ref, near_ref, sem)
    copy.start()
    attend_self(sizes, q_ref, k_ref, v_ref, num_ref, sum_ref, True)
    copy.wait()


def rest_kernel(sizes, *refs):
    frames, share, width, tokens = sizes.frames, sizes.share, sizes.width, sizes.tokens
    count = frames * share
    mine, other = refs[:count], refs[count : 2 * count]
    (
        embed_ref, rows_ref, weight_ref, q_ref, hidden_ref, num_in_ref, sum_in_ref,
        out_weight_ref, final_weight_ref,
    ) = refs[2 * count : 2 * count + 9]
    velocity_refs = refs[2 * count + 9 : 2 * count + 9 + frames]
    updated_refs = refs[2 * count + 9 + frames : 2 * count + 9 + 2 * frames]
    (
        position_scr, latents_scr, normed_scr, proj_scr, k_scr, num_ref, sum_ref,
        text_scr, tk_scr, tv_scr, tnum_scr, tsum_scr, attention_scr,
    ) = refs[2 * count + 9 + 2 * frames :]
    sums_matrix, spread_matrix = head_sums(sizes), head_spread(sizes)
    num_ref[...] = num_in_ref[...]
    sum_ref[...] = sum_in_ref[...]
    for group in range(1, share):
        for block in range(frames):
            at = group * frames + block
            unpack(sizes, block, mine[at], other[at], position_scr, latents_scr)
        embed_blocks(
            sizes, frames, position_scr, latents_scr, embed_ref, rows_ref, normed_scr, None
        )
        project(normed_scr, weight_ref, width, 3 * width, proj_scr)
        keys, values = proj_scr.at[:, :width], proj_scr.at[:, width:]
        norm_rows(sizes, keys, k_scr, rows_ref[6:7, :], sums_matrix, spread_matrix)
        attend_self(sizes, q_ref, k_scr, values, num_ref, sum_ref, False)

    place = lax.axis_index("seq")
    for at in range(count):
        unpack_text(sizes, jnp.bitwise_xor(place, at), mine[at], other[at], text_scr)
    gain_column = jnp.transpose(jnp.broadcast_to(rows_ref[6:7, :], (LANES, width)))[:, 0:1]
    for h in range(sizes.heads):
        rows = slice(h * sizes.head, (h + 1) * sizes.head)
        values = text_scr[0, rows, :]
        mean = jnp.mean(values * values, axis=0, keepdims=True)
        text_scr[0, rows, :] = values * lax.rsqrt(mean + EPSILON) * gain_column[rows]
    tk_scr[...] = text_scr[0].astype(BF16)
    tv_scr[...] = text_scr[1].astype(BF16)
    attend_text(sizes, q_ref, tk_scr, tv_scr, tnum_scr, tsum_scr)

    for start in range(0, sizes.queries, LANES):
        rows = slice(start, start + LANES)
        used = lane_mask((LANES, LANES), 0, sizes.heads)
        own = spread(jnp.where(used, 1.0 / sum_ref[rows, :], 0.0), spread_matrix)
        text = spread(jnp.where(used, 1.0 / tsum_scr[rows, :], 0.0), spread_matrix)
        attention_scr[rows, :] = (num_ref[rows, :] * own + tnum_scr[rows, :] * text).astype(BF16)
    num_ref[...] = dot(attention_scr[...], out_weight_ref[...])
    for block in range(frames):
        rows = slice(block * tokens, (block + 1) * tokens)
        hidden = hidden_ref[rows, :] + rows_ref[2:3, :] * num_ref[rows, :]
        normed = normalize(hidden, rows_ref[4:5, :], rows_ref[3:4, :])
        velocity = dot(final_weight_ref[...], normed, NT)
        velocity_refs[block][...] = velocity
        updated_refs[block][...] = own_latents(sizes, mine[block]) + rows_ref[7:8, :tokens] * velocity


def finish_kernel(sizes, step_ref, levels_ref, latents_ref, noise_ref, *refs):
    frames = sizes.frames
    arrived, next_ones = refs[:frames], refs[frames : 2 * frames]
    advanced_ref, velocity_ref = refs[2 * frames :]
    own_frame = lax.rem(lax.axis_index("seq"), frames)
    for d in range(frames):
        velocity_ref[jnp.bitwise_xor(own_frame, d)] = arrived[d][...]
    for frame in range(1, frames):
        index = step_ref[frame]
        size = levels_ref[index + 1] - levels_ref[index]
        advanced_ref[frame - 1] = latents_ref[frame] + size * velocity_ref[frame]
    after = next_ones[0][...]
    for d in range(1, frames):
        after = jnp.where(own_frame == d, next_ones[d][...], after)
    at_end = lax.axis_index("queue") == lax.axis_size("queue") - 1
    advanced_ref[frames - 1] = jnp.where(at_end, noise_ref[...], after)


def kernel(function, sizes, name, places, outs, scratch, us):
    spaces = {"v": pltpu.VMEM, "h": pltpu.HBM, "s": pltpu.SMEM}
    return pl.pallas_call(
        functools.partial(function, sizes),
        out_shape=outs,
        in_specs=[pl.BlockSpec(memory_space=spaces[place]) for place in places],
        out_specs=jax.tree.map(lambda _: pl.BlockSpec(memory_space=pltpu.VMEM), outs),
        scratch_shapes=scratch,
        compiler_params=pltpu.CompilerParams(vmem_limit_bytes=VMEM_LIMIT),
        cost_estimate=pl.CostEstimate(
            flops=int(us * 1e9), bytes_accessed=int(us * 1e6), transcendentals=0
        ),
        name=name,
    )


def body(
    latents,
    step_index,
    levels,
    modulation,
    embed_weight,
    position,
    qkv_weight,
    q_gain,
    k_gain,
    text_kv,
    out_weight,
    final_weight,
    new_noise,
):
    text = jnp.swapaxes(text_kv, 1, 2)
    modulation = jnp.swapaxes(modulation, 0, 1)
    sizes = Sizes(latents, position, text, q_gain, lax.axis_size("seq"))
    frames, width, tokens, queries = sizes.frames, sizes.width, sizes.tokens, sizes.queries
    queue = lax.axis_size("queue")

    def swapped(value, d):
        return lax.ppermute(value, "seq", [(i, i ^ d) for i in range(sizes.seq)])

    def over_cores(value):
        return lax.ppermute(value, "queue", [(i, i ^ 1) for i in range(queue)])

    far = functools.partial(pltpu.with_memory_space_constraint, memory_space=pltpu.HBM)

    payload = kernel(
        prep_kernel,
        sizes,
        "prep",
        "hhh",
        pltpu.VMEM((ROWS, sizes.payload), BF16),
        [
            pltpu.VMEM(latents.shape, F32),
            pltpu.VMEM(text.shape[1:], BF16),
            pltpu.SemaphoreType.DMA((2 + sizes.pieces,)),
        ],
        1.5,
    )(far(position), far(latents), far(text))

    direct = [swapped(payload, d) for d in range(1, frames)]
    direct += [swapped(payload, group * frames) for group in range(1, sizes.share)]
    payload_other = over_cores(payload)

    def blocks(count):
        return [
            pltpu.VMEM((count * tokens, width), BF16),
            pltpu.VMEM((2 * ROWS, count * tokens), BF16),
            pltpu.VMEM((count * tokens, width), BF16),
        ]

    def token_arrays(count):
        rows = count * tokens
        return [pltpu.VMEM((rows, width), BF16)] * 3 + [pltpu.VMEM((rows, width), F32)]

    rows, near_qkv, *one = kernel(
        first_kernel,
        sizes,
        "first",
        "ssvvvvvvh",
        [pltpu.VMEM((8, width), F32), pltpu.VMEM(qkv_weight.shape, BF16)] + token_arrays(1),
        blocks(1) + [pltpu.VMEM((tokens, width), BF16), pltpu.SemaphoreType.DMA((3,))],
        4,
    )(
        step_index,
        levels,
        modulation,
        q_gain[None],
        k_gain[None],
        payload,
        payload_other,
        embed_weight,
        far(qkv_weight),
    )
    rows, *direct = lax.optimization_barrier((rows, *direct))
    square, far_blocks = direct[: frames - 1], direct[frames - 1 :]
    square_other = [over_cores(value) for value in square]
    beyond = [far_blocks] + [[swapped(v, d) for v in far_blocks] for d in range(1, frames)]
    beyond = [beyond[d][group] for group in range(sizes.share - 1) for d in range(frames)]
    q_hat, k_hat, value, hidden = kernel(
        own_kernel,
        sizes,
        "own",
        "v" * (2 * (frames - 1) + 7),
        token_arrays(frames),
        blocks(frames - 1) + [pltpu.VMEM(((frames - 1) * tokens, 2 * width), BF16)],
        8,
    )(*square, *square_other, embed_weight, rows, near_qkv, *one)
    sums_shape = pltpu.VMEM((queries, LANES), F32)
    num, sums, near_out = kernel(
        attend_kernel,
        sizes,
        "attend",
        "vvvh",
        [pltpu.VMEM((queries, width), F32), sums_shape, pltpu.VMEM(out_weight.shape, BF16)],
        [pltpu.SemaphoreType.DMA],
        5,
    )(q_hat, k_hat, value, far(out_weight))
    num, *beyond = lax.optimization_barrier((num, *beyond))
    mine = [payload, *square, *beyond]
    other = [payload_other, *square_other] + [over_cores(value) for value in beyond]
    results = kernel(
        rest_kernel,
        sizes,
        "rest",
        "v" * (2 * sizes.seq + 9),
        [pltpu.VMEM((sizes.channels, tokens), F32)] * (2 * frames),
        blocks(frames)
        + [pltpu.VMEM((queries, 2 * width), BF16), pltpu.VMEM((queries, width), BF16)]
        + [
            pltpu.VMEM((queries, width), F32),
            sums_shape,
            pltpu.VMEM((2, width, sizes.text_len), F32),
            pltpu.VMEM((width, sizes.text_len), BF16),
            pltpu.VMEM((width, sizes.text_len), BF16),
            pltpu.VMEM((queries, width), F32),
            sums_shape,
            pltpu.VMEM((queries, width), BF16),
        ],
        18,
    )(
        *mine,
        *other,
        embed_weight,
        rows,
        near_qkv,
        q_hat,
        hidden,
        num,
        sums,
        near_out,
        final_weight.T,
    )

    velocities, updated = results[:frames], results[frames:]

    def to_previous(value, d):
        route = [
            (q * sizes.seq + i, (q - 1) * sizes.seq + (i ^ d))
            for q in range(1, queue)
            for i in range(0, sizes.seq, frames)
        ]
        return lax.ppermute(value, ("queue", "seq"), route)

    arrived = [velocities[0]] + [swapped(velocities[d], d) for d in range(1, frames)]
    next_ones = [to_previous(updated[d], d) for d in range(frames)]
    whole = jax.ShapeDtypeStruct(latents.shape, F32)
    return tuple(
        kernel(finish_kernel, sizes, "finish", "ss" + "v" * (2 + 2 * frames), [whole, whole], [], 1)(
            step_index, levels, latents, new_noise, *arrived, *next_ones
        )
    )


def solution(mesh):
    in_specs = (
        P("queue", None, "seq"),
        P("queue"),
        P(),
        P(),
        P(),
        P("seq", None),
        P(),
        P(),
        P(),
        P(None, None, "seq"),
        P(),
        P(),
        P(None, "seq"),
    )
    out_specs = (P("queue", None, "seq"), P("queue", None, "seq"))
    return jax.shard_map(body, mesh=mesh, in_specs=in_specs, out_specs=out_specs, check_vma=False)
```

```python
import functools
import math

import jax
import jax.numpy as jnp
from jax import lax
from jax.experimental import pallas as pl
from jax.experimental.pallas import tpu as pltpu
from jax.sharding import PartitionSpec as P

EPSILON = 1e-06
LANES = 128
ROWS = 16
F32 = jnp.float32
BF16 = jnp.bfloat16
VMEM_LIMIT = 24 * 1024 * 1024
NN = (((1,), (0,)), ((), ()))
NT = (((1,), (1,)), ((), ()))
TN = (((0,), (0,)), ((), ()))


def dot(a, b, dims=NN):
    return lax.dot_general(a, b, dims, preferred_element_type=F32)


def split_parts(values):
    high = values.astype(BF16)
    low = (values - high.astype(F32)).astype(BF16)
    return high, low


class Sizes:
    def __init__(self, latents, position, text, q_gain, seq):
        self.frames, self.channels, self.tokens = latents.shape
        self.width = position.shape[1]
        self.head = q_gain.shape[0]
        self.heads = self.width // self.head
        self.seq = seq
        self.share = seq // self.frames
        self.queries = self.frames * self.tokens
        _, self.part, self.text_len = text.shape
        self.half = self.tokens // 2
        self.pieces = self.half // ROWS
        self.text_pieces = -(-self.part // ROWS)
        self.latents_at = self.pieces * self.width
        self.text_at = self.latents_at + 2 * self.frames * self.tokens
        self.payload = self.text_at + self.text_pieces * self.text_len
        self.near = self.latents_at + 2 * self.tokens


def prep_kernel(sizes, position_ref, latents_ref, text_ref, payload_ref, tail_ref, *refs):
    near_refs, (latents_scr, text_scr, sems) = refs[:-3], refs[-3:]
    core = lax.rem(lax.axis_index("queue"), 2)
    width, tokens = sizes.width, sizes.tokens
    copies = [
        pltpu.make_async_copy(latents_ref, latents_scr, sems.at[0]),
        pltpu.make_async_copy(text_ref.at[core], text_scr, sems.at[1]),
    ]
    for piece in range(sizes.pieces):
        start = pl.multiple_of(core * sizes.half + piece * ROWS, ROWS)
        copies.append(
            pltpu.make_async_copy(
                position_ref.at[pl.ds(start, ROWS), :],
                payload_ref.at[:, piece * width : (piece + 1) * width],
                sems.at[2 + piece],
            )
        )
    for copy in copies:
        copy.start()
    copies[0].wait()
    for frame in range(sizes.frames):
        high, low = split_parts(latents_scr[frame])
        at = sizes.latents_at + 2 * frame * tokens
        payload_ref[:, at : at + tokens] = high
        payload_ref[:, at + tokens : at + 2 * tokens] = low
    copies[1].wait()
    for piece in range(sizes.text_pieces):
        first, last = piece * ROWS, min((piece + 1) * ROWS, sizes.part)
        rows = text_scr[first:last, :]
        if last - first < ROWS:
            blank = jnp.zeros((ROWS - (last - first), sizes.text_len), BF16)
            rows = jnp.concatenate([rows, blank], axis=0)
        at = sizes.text_at + piece * sizes.text_len
        payload_ref[:, at : at + sizes.text_len] = rows
        tail_ref[:, piece * sizes.text_len : (piece + 1) * sizes.text_len] = rows
    for copy in copies[2:]:
        copy.wait()
    own_frame = lax.rem(lax.axis_index("seq"), sizes.frames)
    base = sizes.latents_at
    for d, near_ref in enumerate(near_refs, 1):
        near_ref[:, :base] = payload_ref[:, :base]
        at = base + 2 * tokens * jnp.bitwise_xor(own_frame, d)
        near_ref[:, base:] = payload_ref[:, pl.ds(pl.multiple_of(at, LANES), 2 * tokens)]


def join_kernel(sizes, far_ref, tail_ref, joined_ref):
    joined_ref[:, : sizes.payload] = far_ref[...]
    joined_ref[:, sizes.payload :] = tail_ref[...]


def frame_latents(sizes, mine_ref):
    if mine_ref.shape[1] == sizes.near:
        return mine_ref[:, sizes.latents_at :]
    frame = lax.rem(lax.axis_index("seq"), sizes.frames)
    at = pl.multiple_of(sizes.latents_at + 2 * frame * sizes.tokens, LANES)
    return mine_ref[:, pl.ds(at, 2 * sizes.tokens)]


def unpack(sizes, block, mine_ref, other_ref, position_scr, latents_scr):
    width, tokens = sizes.width, sizes.tokens
    core = lax.rem(lax.axis_index("queue"), 2)
    for ref, place in ((mine_ref, core), (other_ref, 1 - core)):
        for piece in range(sizes.pieces):
            start = pl.multiple_of(block * tokens + place * sizes.half + piece * ROWS, ROWS)
            position_scr[pl.ds(start, ROWS), :] = ref[:, piece * width : (piece + 1) * width]
    both = frame_latents(sizes, mine_ref)
    lanes = slice(block * tokens, (block + 1) * tokens)
    latents_scr[0:ROWS, lanes] = both[:, :tokens]
    latents_scr[ROWS : 2 * ROWS, lanes] = both[:, tokens:]


def unpack_text(sizes, shard, mine_ref, other_ref, base, text_scr):
    core = lax.rem(lax.axis_index("queue"), 2)
    for ref, place in ((mine_ref, core), (other_ref, 1 - core)):
        for piece in range(sizes.text_pieces):
            first, last = piece * ROWS, min((piece + 1) * ROWS, sizes.part)
            at = base + piece * sizes.text_len
            rows = ref[:, at : at + sizes.text_len].astype(F32)
            start = pl.multiple_of(shard * sizes.part + first, 8)
            text_scr[place, pl.ds(start, last - first), :] = rows[: last - first]


def normalize(values, scale, shift):
    center = values - jnp.mean(values, axis=-1, keepdims=True)
    variance = jnp.mean(center * center, axis=-1, keepdims=True)
    return (center * lax.rsqrt(variance + EPSILON) * scale + shift).astype(BF16)


def embed_blocks(sizes, blocks, position_scr, latents_scr, embed_ref, rows_ref, normed_scr, hidden):
    tokens = sizes.tokens
    embed = jnp.concatenate([embed_ref[...], embed_ref[...]], axis=0)
    embedded = dot(latents_scr[...], embed, TN)
    for block in range(blocks):
        rows = slice(block * tokens, (block + 1) * tokens)
        values = embedded[rows] + position_scr[rows, :].astype(F32)
        if hidden is not None:
            hidden[rows, :] = values
        normed_scr[rows, :] = normalize(values, rows_ref[1:2, :], rows_ref[0:1, :])


def head_sums(sizes):
    column = lax.broadcasted_iota(jnp.int32, (sizes.width, LANES), 0)
    first = lax.broadcasted_iota(jnp.int32, (sizes.width, LANES), 1) * sizes.head
    inside = (column >= first) & (column < first + sizes.head)
    return jnp.where(inside, 1.0, 0.0).astype(BF16)


def head_spread(sizes):
    column = lax.broadcasted_iota(jnp.int32, (LANES, sizes.width), 1)
    first = lax.broadcasted_iota(jnp.int32, (LANES, sizes.width), 0) * sizes.head
    inside = (column >= first) & (column < first + sizes.head)
    one = jnp.where(inside, 1.0, 0.0).astype(BF16)
    return jnp.concatenate([one, one], axis=0)


def spread(values, spread_matrix):
    high, low = split_parts(values)
    return dot(jnp.concatenate([high, low], axis=1), spread_matrix)


def norm_rows(sizes, source, target, gain, sums_matrix, spread_matrix, step=256):
    for start in range(0, source.shape[0], step):
        wide = source[start : start + step, :].astype(F32)
        squares = dot((wide * wide).astype(BF16), sums_matrix) * (1.0 / sizes.head)
        factor = spread(lax.rsqrt(squares + EPSILON), spread_matrix)
        target[start : start + step, :] = (wide * factor * gain).astype(BF16)


def project(normed_scr, weight_ref, first, last, out_ref, chunk=256):
    for start in range(first, last, chunk):
        end = min(start + chunk, last)
        out_ref[:, start - first : end - first] = dot(
            normed_scr[...], weight_ref[:, start:end]
        ).astype(BF16)


def window(first, last, width):
    start = first // LANES * LANES
    end = min(-(-last // LANES) * LANES, width)
    return start, end


def lane_mask(shape, first, last, axis=1):
    lane = lax.broadcasted_iota(jnp.int32, shape, axis)
    return (lane >= first) & (lane < last)


def keep(values, first, last, axis=1):
    inside = lane_mask(values.shape, first, last, axis)
    return jnp.where(inside, values, jnp.zeros_like(values))


def attend_self(sizes, q_ref, k_ref, v_ref, num_ref, sum_ref, fresh, q_step=512):
    queries, width = q_ref.shape
    keys = k_ref.shape[0]
    q_step = min(q_step, queries)
    for q_start in range(0, queries, q_step):
        rows = slice(q_start, q_start + q_step)
        sums = jnp.zeros((q_step, LANES), F32)
        pending = jnp.zeros((q_step, LANES), F32)
        for h in range(sizes.heads):
            first, last = h * sizes.head, (h + 1) * sizes.head
            start, end = window(first, last, width)
            span = (first - start, last - start)
            scores = dot(keep(q_ref[rows, start:end], *span), k_ref[:, start:end], NT)
            weights = jnp.exp2(scores).astype(BF16)
            v = keep(v_ref[:, start:end], *span)
            mark = lane_mask((keys, LANES), h, h + 1)
            if end - start == LANES:
                ones = jnp.where(mark, 1.0, 0.0).astype(BF16)
                both = dot(weights, jnp.concatenate([v, ones], axis=1))
                sums = sums + both[:, LANES:]
                pending = pending + both[:, :LANES]
            else:
                lead = jnp.where(mark, jnp.ones((), BF16), v[:, :LANES])
                both = dot(weights, jnp.concatenate([lead, v[:, LANES:]], axis=1))
                tops = lane_mask((q_step, LANES), 0, sizes.heads)
                left = both[:, :LANES]
                sums = sums + jnp.where(tops, left, 0.0)
                pending = pending + jnp.where(tops, 0.0, left)
            if last >= start + LANES:
                if fresh:
                    num_ref[rows, start : start + LANES] = pending
                else:
                    num_ref[rows, start : start + LANES] += pending
                wide = end - start > LANES
                pending = both[:, LANES:] if wide else jnp.zeros((q_step, LANES), F32)
        if fresh:
            sum_ref[rows, :] = sums
        else:
            sum_ref[rows, :] += sums


def attend_text(sizes, q_ref, k_scr, v_scr, num_ref, sum_ref, q_step=512):
    queries, width = q_ref.shape
    keys = k_scr.shape[1]
    for q_start in range(0, queries, q_step):
        rows = slice(q_start, q_start + q_step)
        sums = jnp.zeros((q_step, LANES), F32)
        pending, pending_at = None, None
        for pair in range(0, sizes.heads, 2):
            edges = [(pair + i) * sizes.head for i in range(3)]
            start, end = window(edges[0], edges[2], width)
            spans = [(edges[i] - start, edges[i + 1] - start) for i in range(2)]
            k = jnp.concatenate([keep(k_scr[start:end, :], *span, 0) for span in spans], axis=1)
            v = jnp.concatenate([keep(v_scr[start:end, :], *span, 0) for span in spans], axis=1)
            ones = [
                jnp.where(lane_mask((keys, LANES), h, h + 1), 1.0, 0.0).astype(BF16)
                for h in (pair, pair + 1)
            ]
            weights = jnp.exp2(dot(q_ref[rows, start:end], k)).astype(BF16)
            both = dot(weights, v, NT)
            sums = sums + dot(weights, jnp.concatenate(ones, axis=0))
            for at in range(start, end, LANES):
                part = both[:, at - start : at - start + LANES]
                if pending_at == at:
                    part = pending + part
                elif pending_at is not None and pending_at < at:
                    num_ref[rows, pending_at : pending_at + LANES] = pending
                pending, pending_at = part, at
        num_ref[rows, pending_at : pending_at + LANES] = pending
        sum_ref[rows, :] = sums


def first_kernel(
    sizes, step_ref, levels_ref, modulation_ref, q_gain_ref, k_gain_ref, mine, other, embed_ref, weight_ref,
    rows_ref, near_ref, q_ref, k_ref, v_ref, hidden_ref,
    position_scr, latents_scr, normed_scr, proj_scr, sems,
):
    width = sizes.width
    copies = []
    for i in range(3):
        columns = slice(i * width, (i + 1) * width)
        copies.append(
            pltpu.make_async_copy(
                weight_ref.at[:, columns], near_ref.at[:, columns], sems.at[i]
            )
        )
        copies[i].start()
    frame = lax.rem(lax.axis_index("seq"), sizes.frames)
    index = step_ref[frame]
    for i in range(5):
        row = modulation_ref[i, pl.ds(index, 1), :]
        rows_ref[i : i + 1, :] = row + 1.0 if i in (1, 4) else row
    factor = math.log2(math.e) / math.sqrt(sizes.head)
    for h in range(sizes.heads):
        rows_ref[5:6, h * sizes.head : (h + 1) * sizes.head] = q_gain_ref[...] * factor
        rows_ref[6:7, h * sizes.head : (h + 1) * sizes.head] = k_gain_ref[...]
    rows_ref[7:8, :] = jnp.full((1, width), levels_ref[index + 1] - levels_ref[index])
    unpack(sizes, 0, mine, other, position_scr, latents_scr)
    embed_blocks(
        sizes, 1, position_scr, latents_scr, embed_ref, rows_ref, normed_scr, hidden_ref
    )
    matrices = head_sums(sizes), head_spread(sizes)
    copies[0].wait()
    project(normed_scr, near_ref, 0, width, proj_scr)
    norm_rows(sizes, proj_scr, q_ref, rows_ref[5:6, :], *matrices)
    copies[1].wait()
    project(normed_scr, near_ref, width, 2 * width, proj_scr)
    norm_rows(sizes, proj_scr, k_ref, rows_ref[6:7, :], *matrices)
    copies[2].wait()
    project(normed_scr, near_ref, 2 * width, 3 * width, v_ref)


def own_kernel(sizes, *refs):
    count = sizes.frames - 1
    mine, other = refs[:count], refs[count : 2 * count]
    (
        embed_ref, rows_ref, weight_ref, q_one, k_one, v_one, hidden_one,
        q_ref, k_ref, v_ref, hidden_ref, position_scr, latents_scr, normed_scr, proj_scr,
    ) = refs[2 * count :]
    width, tokens = sizes.width, sizes.tokens
    for block in range(count):
        unpack(sizes, block, mine[block], other[block], position_scr, latents_scr)
    q_ref[:tokens, :] = q_one[...]
    k_ref[:tokens, :] = k_one[...]
    v_ref[:tokens, :] = v_one[...]
    hidden_ref[:tokens, :] = hidden_one[...]
    embed_blocks(
        sizes, count, position_scr, latents_scr, embed_ref, rows_ref, normed_scr,
        hidden_ref.at[tokens:, :],
    )
    project(normed_scr, weight_ref, 0, 2 * width, proj_scr)
    project(normed_scr, weight_ref, 2 * width, 3 * width, v_ref.at[tokens:, :])
    matrices = head_sums(sizes), head_spread(sizes)
    norm_rows(
        sizes, proj_scr.at[:, :width], q_ref.at[tokens:, :], rows_ref[5:6, :], *matrices
    )
    norm_rows(
        sizes, proj_scr.at[:, width:], k_ref.at[tokens:, :], rows_ref[6:7, :], *matrices
    )


def attend_kernel(sizes, q_ref, k_ref, v_ref, out_weight_ref, num_ref, sum_ref, near_ref, sem):
    copy = pltpu.make_async_copy(out_weight_ref, near_ref, sem)
    copy.start()
    attend_self(sizes, q_ref, k_ref, v_ref, num_ref, sum_ref, True)
    copy.wait()


def far_kernel(sizes, *refs):
    count, width = sizes.share - 1, sizes.width
    mine, other = refs[:count], refs[count : 2 * count]
    (
        embed_ref, rows_ref, weight_ref, k_ref, v_ref,
        position_scr, latents_scr, normed_scr, proj_scr,
    ) = refs[2 * count :]
    for block in range(count):
        unpack(sizes, block, mine[block], other[block], position_scr, latents_scr)
    embed_blocks(
        sizes, count, position_scr, latents_scr, embed_ref, rows_ref, normed_scr, None
    )
    project(normed_scr, weight_ref, width, 2 * width, proj_scr)
    norm_rows(sizes, proj_scr, k_ref, rows_ref[6:7, :], head_sums(sizes), head_spread(sizes))
    project(normed_scr, weight_ref, 2 * width, 3 * width, v_ref)


def rest_kernel(sizes, *refs):
    frames, share, width, tokens = sizes.frames, sizes.share, sizes.width, sizes.tokens
    count = frames * (share - 1)
    mine, other = refs[:count], refs[count : 2 * count]
    refs = refs[2 * count :]
    payload_ref, payload_other_ref = refs[:2]
    square = refs[2 : 1 + frames]
    (
        embed_ref, rows_ref, weight_ref, q_ref, hidden_ref, num_in_ref, sum_in_ref,
        out_weight_ref, final_weight_ref, far_k_ref, far_v_ref,
    ) = refs[1 + frames : 12 + frames]
    refs = refs[12 + frames :]
    velocity_refs = refs[:frames]
    updated_refs = refs[frames : 2 * frames]
    (
        position_scr, latents_scr, normed_scr, proj_scr, k_scr, v_scr, num_ref, sum_ref,
        text_scr, tk_scr, tv_scr, tnum_scr, tsum_scr, attention_scr,
    ) = refs[2 * frames :]
    sums_matrix, spread_matrix = head_sums(sizes), head_spread(sizes)
    num_ref[...] = num_in_ref[...]
    sum_ref[...] = sum_in_ref[...]
    for group in range(share - 1):
        first = slice(group * tokens, (group + 1) * tokens)
        k_scr[:tokens, :] = far_k_ref[first, :]
        v_scr[:tokens, :] = far_v_ref[first, :]
        for block in range(1, frames):
            at = group * frames + block
            unpack(sizes, block - 1, mine[at], other[at], position_scr, latents_scr)
        embed_blocks(
            sizes, frames - 1, position_scr, latents_scr, embed_ref, rows_ref, normed_scr, None
        )
        project(normed_scr, weight_ref, width, 2 * width, proj_scr)
        project(normed_scr, weight_ref, 2 * width, 3 * width, v_scr.at[tokens:, :])
        keys = k_scr.at[tokens:, :]
        norm_rows(sizes, proj_scr, keys, rows_ref[6:7, :], sums_matrix, spread_matrix)
        attend_self(sizes, q_ref, k_scr, v_scr, num_ref, sum_ref, False)

    place = lax.axis_index("seq")
    unpack_text(sizes, place, payload_ref, payload_other_ref, sizes.text_at, text_scr)
    for d in range(1, frames):
        shard = jnp.bitwise_xor(place, d)
        unpack_text(sizes, shard, mine[d], other[d], sizes.payload, text_scr)
    for at in range(count):
        shard = jnp.bitwise_xor(place, frames + at)
        unpack_text(sizes, shard, mine[at], other[at], sizes.text_at, text_scr)
    gain_column = jnp.transpose(jnp.broadcast_to(rows_ref[6:7, :], (LANES, width)))[:, 0:1]
    for h in range(sizes.heads):
        rows = slice(h * sizes.head, (h + 1) * sizes.head)
        values = text_scr[0, rows, :]
        mean = jnp.mean(values * values, axis=0, keepdims=True)
        text_scr[0, rows, :] = values * lax.rsqrt(mean + EPSILON) * gain_column[rows]
    tk_scr[...] = text_scr[0].astype(BF16)
    tv_scr[...] = text_scr[1].astype(BF16)
    attend_text(sizes, q_ref, tk_scr, tv_scr, tnum_scr, tsum_scr)

    for start in range(0, sizes.queries, LANES):
        rows = slice(start, start + LANES)
        used = lane_mask((LANES, LANES), 0, sizes.heads)
        own = spread(jnp.where(used, 1.0 / sum_ref[rows, :], 0.0), spread_matrix)
        text = spread(jnp.where(used, 1.0 / tsum_scr[rows, :], 0.0), spread_matrix)
        attention_scr[rows, :] = (num_ref[rows, :] * own + tnum_scr[rows, :] * text).astype(BF16)
    num_ref[...] = dot(attention_scr[...], out_weight_ref[...])
    for block in range(frames):
        rows = slice(block * tokens, (block + 1) * tokens)
        hidden = hidden_ref[rows, :] + rows_ref[2:3, :] * num_ref[rows, :]
        normed = normalize(hidden, rows_ref[4:5, :], rows_ref[3:4, :])
        velocity = dot(final_weight_ref[...], normed, NT)
        velocity_refs[block][...] = velocity
        both = frame_latents(sizes, square[block - 1] if block else payload_ref).astype(F32)
        before = both[:, :tokens] + both[:, tokens:]
        updated_refs[block][...] = before + rows_ref[7:8, :tokens] * velocity


def finish_kernel(sizes, step_ref, levels_ref, latents_ref, noise_ref, *refs):
    frames = sizes.frames
    arrived, next_ones = refs[:frames], refs[frames : 2 * frames]
    advanced_ref, velocity_ref = refs[2 * frames :]
    own_frame = lax.rem(lax.axis_index("seq"), frames)
    for d in range(frames):
        velocity_ref[jnp.bitwise_xor(own_frame, d)] = arrived[d][...]
    for frame in range(1, frames):
        index = step_ref[frame]
        size = levels_ref[index + 1] - levels_ref[index]
        advanced_ref[frame - 1] = latents_ref[frame] + size * velocity_ref[frame]
    after = next_ones[0][...]
    for d in range(1, frames):
        after = jnp.where(own_frame == d, next_ones[d][...], after)
    at_end = lax.axis_index("queue") == lax.axis_size("queue") - 1
    advanced_ref[frames - 1] = jnp.where(at_end, noise_ref[...], after)


def kernel(function, sizes, name, places, outs, scratch, us):
    spaces = {"v": pltpu.VMEM, "h": pltpu.HBM, "s": pltpu.SMEM}
    return pl.pallas_call(
        functools.partial(function, sizes),
        out_shape=outs,
        in_specs=[pl.BlockSpec(memory_space=spaces[place]) for place in places],
        out_specs=jax.tree.map(lambda _: pl.BlockSpec(memory_space=pltpu.VMEM), outs),
        scratch_shapes=scratch,
        compiler_params=pltpu.CompilerParams(vmem_limit_bytes=VMEM_LIMIT),
        cost_estimate=pl.CostEstimate(
            flops=int(us * 1e9), bytes_accessed=int(us * 1e6), transcendentals=0
        ),
        name=name,
    )


def body(
    latents,
    step_index,
    levels,
    modulation,
    embed_weight,
    position,
    qkv_weight,
    q_gain,
    k_gain,
    text_kv,
    out_weight,
    final_weight,
    new_noise,
):
    text = jnp.swapaxes(text_kv, 1, 2)
    modulation = jnp.swapaxes(modulation, 0, 1)
    sizes = Sizes(latents, position, text, q_gain, lax.axis_size("seq"))
    frames, width, tokens, queries = sizes.frames, sizes.width, sizes.tokens, sizes.queries
    queue = lax.axis_size("queue")

    def swapped(value, d):
        return lax.ppermute(value, "seq", [(i, i ^ d) for i in range(sizes.seq)])

    def over_cores(value):
        return lax.ppermute(value, "queue", [(i, i ^ 1) for i in range(queue)])

    far = functools.partial(pltpu.with_memory_space_constraint, memory_space=pltpu.HBM)

    payload, tail, *near = kernel(
        prep_kernel,
        sizes,
        "prep",
        "hhh",
        [
            pltpu.VMEM((ROWS, sizes.payload), BF16),
            pltpu.VMEM((ROWS, sizes.payload - sizes.text_at), BF16),
        ]
        + [pltpu.VMEM((ROWS, sizes.near), BF16)] * (frames - 1),
        [
            pltpu.VMEM(latents.shape, F32),
            pltpu.VMEM(text.shape[1:], BF16),
            pltpu.SemaphoreType.DMA((2 + sizes.pieces,)),
        ],
        1.5,
    )(far(position), far(latents), far(text))

    order = sorted(range(1, frames), key=lambda d: (d.bit_count() - 2 * (d >= frames // 2), d))
    sent = {d: swapped(near[d - 1], d) for d in order}
    direct = [sent[d] for d in range(1, frames)]
    payload_other = over_cores(payload)
    late, payload_other = lax.optimization_barrier((payload, payload_other))
    direct += [swapped(late, group * frames) for group in range(1, sizes.share)]

    def blocks(count):
        return [
            pltpu.VMEM((count * tokens, width), BF16),
            pltpu.VMEM((2 * ROWS, count * tokens), BF16),
            pltpu.VMEM((count * tokens, width), BF16),
        ]

    def token_arrays(count):
        rows = count * tokens
        return [pltpu.VMEM((rows, width), BF16)] * 3 + [pltpu.VMEM((rows, width), F32)]

    rows, near_qkv, *one = kernel(
        first_kernel,
        sizes,
        "first",
        "ssvvvvvvh",
        [pltpu.VMEM((8, width), F32), pltpu.VMEM(qkv_weight.shape, BF16)] + token_arrays(1),
        blocks(1) + [pltpu.VMEM((tokens, width), BF16), pltpu.SemaphoreType.DMA((3,))],
        4,
    )(
        step_index,
        levels,
        modulation,
        q_gain[None],
        k_gain[None],
        payload,
        payload_other,
        embed_weight,
        far(qkv_weight),
    )
    rows, *direct = lax.optimization_barrier((rows, *direct))
    square, far_blocks = direct[: frames - 1], direct[frames - 1 :]
    square_other = [over_cores(value) for value in square]
    far_other = [over_cores(value) for value in far_blocks]
    joined = [
        kernel(
            join_kernel,
            sizes,
            "join",
            "vv",
            pltpu.VMEM((ROWS, 2 * sizes.payload - sizes.text_at), BF16),
            [],
            0.3,
        )(value, tail)
        for value in far_blocks
    ]
    forwarded = [[swapped(value, d) for d in range(1, frames)] for value in joined]
    forwarded = sum(forwarded, [])
    q_hat, k_hat, value, hidden = kernel(
        own_kernel,
        sizes,
        "own",
        "v" * (2 * (frames - 1) + 7),
        token_arrays(frames),
        blocks(frames - 1) + [pltpu.VMEM(((frames - 1) * tokens, 2 * width), BF16)],
        8,
    )(*square, *square_other, embed_weight, rows, near_qkv, *one)
    num, sums, near_out = kernel(
        attend_kernel,
        sizes,
        "attend",
        "vvvh",
        [
            pltpu.VMEM((queries, width), F32),
            pltpu.VMEM((queries, LANES), F32),
            pltpu.VMEM(out_weight.shape, BF16),
        ],
        [pltpu.SemaphoreType.DMA],
        5,
    )(q_hat, k_hat, value, far(out_weight))
    num, rows_late, *forwarded = lax.optimization_barrier((num, rows, *forwarded))
    forwarded_other = [over_cores(value) for value in forwarded]
    far_rows = (sizes.share - 1) * tokens
    far_k, far_v = kernel(
        far_kernel,
        sizes,
        "far",
        "v" * (2 * len(far_blocks) + 3),
        [pltpu.VMEM((far_rows, width), BF16)] * 2,
        blocks(sizes.share - 1) + [pltpu.VMEM((far_rows, width), BF16)],
        2.5,
    )(*far_blocks, *far_other, embed_weight, rows_late, near_qkv)
    mine, other = [], []
    for group in range(sizes.share - 1):
        here = slice(group * (frames - 1), (group + 1) * (frames - 1))
        mine += [far_blocks[group], *forwarded[here]]
        other += [far_other[group], *forwarded_other[here]]
    results = kernel(
        rest_kernel,
        sizes,
        "rest",
        "v" * (2 * len(mine) + 12 + frames),
        [pltpu.VMEM((sizes.channels, tokens), F32)] * (2 * frames),
        blocks(frames - 1)
        + [pltpu.VMEM(((frames - 1) * tokens, width), BF16)]
        + [pltpu.VMEM((queries, width), BF16)] * 2
        + [
            pltpu.VMEM((queries, width), F32),
            pltpu.VMEM((queries, LANES), F32),
            pltpu.VMEM((2, width, sizes.text_len), F32),
            pltpu.VMEM((width, sizes.text_len), BF16),
            pltpu.VMEM((width, sizes.text_len), BF16),
            pltpu.VMEM((queries, width), F32),
            pltpu.VMEM((queries, LANES), F32),
            pltpu.VMEM((queries, width), BF16),
        ],
        18,
    )(
        *mine,
        *other,
        payload,
        payload_other,
        *square,
        embed_weight,
        rows,
        near_qkv,
        q_hat,
        hidden,
        num,
        sums,
        near_out,
        final_weight.T,
        far_k,
        far_v,
    )

    velocities, updated = results[:frames], results[frames:]

    def to_previous(value, d):
        route = [
            (q * sizes.seq + i, (q - 1) * sizes.seq + (i ^ d))
            for q in range(1, queue)
            for i in range(0, sizes.seq, frames)
        ]
        return lax.ppermute(value, ("queue", "seq"), route)

    arrived = [velocities[0]] + [swapped(velocities[d], d) for d in range(1, frames)]
    next_ones = [to_previous(updated[d], d) for d in range(frames)]
    whole = jax.ShapeDtypeStruct(latents.shape, F32)
    return tuple(
        kernel(finish_kernel, sizes, "finish", "ss" + "v" * (2 + 2 * frames), [whole, whole], [], 1)(
            step_index, levels, latents, new_noise, *arrived, *next_ones
        )
    )


def solution(mesh):
    in_specs = (
        P("queue", None, "seq"),
        P("queue"),
        P(),
        P(),
        P(),
        P("seq", None),
        P(),
        P(),
        P(),
        P(None, None, "seq"),
        P(),
        P(),
        P(None, "seq"),
    )
    out_specs = (P("queue", None, "seq"), P("queue", None, "seq"))
    return jax.shard_map(body, mesh=mesh, in_specs=in_specs, out_specs=out_specs, check_vma=False)
```

```python
import functools
import math

import jax
import jax.numpy as jnp
from jax import lax
from jax.experimental import pallas as pl
from jax.experimental.pallas import tpu as pltpu
from jax.sharding import PartitionSpec as P

EPSILON = 1e-06
LANES = 128
ROWS = 16
F32 = jnp.float32
BF16 = jnp.bfloat16
VMEM_LIMIT = 24 * 1024 * 1024
NN = (((1,), (0,)), ((), ()))
NT = (((1,), (1,)), ((), ()))
TN = (((0,), (0,)), ((), ()))


def dot(a, b, dims=NN):
    return lax.dot_general(a, b, dims, preferred_element_type=F32)


def split_parts(values):
    high = values.astype(BF16)
    low = (values - high.astype(F32)).astype(BF16)
    return high, low


class Sizes:
    def __init__(self, latents, position, text, q_gain, seq):
        self.frames, self.channels, self.tokens = latents.shape
        self.width = position.shape[1]
        self.head = q_gain.shape[0]
        self.heads = self.width // self.head
        self.seq = seq
        self.share = seq // self.frames
        self.queries = self.frames * self.tokens
        _, self.part, self.text_len = text.shape
        self.half = self.tokens // 2
        self.pieces = self.half // ROWS
        self.text_pieces = -(-self.part // ROWS)
        self.latents_at = self.pieces * self.width
        self.text_at = self.latents_at + 2 * self.frames * self.tokens
        self.payload = self.text_at + self.text_pieces * self.text_len
        self.near = self.latents_at + 2 * self.tokens


def prep_kernel(sizes, position_ref, latents_ref, text_ref, payload_ref, mate_ref, tail_ref, *refs):
    near_refs, (latents_scr, text_scr, sems) = refs[:-3], refs[-3:]
    core = lax.rem(lax.axis_index("queue"), 2)
    width, tokens = sizes.width, sizes.tokens
    copies = [
        pltpu.make_async_copy(latents_ref, latents_scr, sems.at[0]),
        pltpu.make_async_copy(text_ref, text_scr, sems.at[1]),
    ]
    for i, (target, place) in enumerate(((payload_ref, core), (mate_ref, 1 - core))):
        for piece in range(sizes.pieces):
            start = pl.multiple_of(place * sizes.half + piece * ROWS, ROWS)
            copies.append(
                pltpu.make_async_copy(
                    position_ref.at[pl.ds(start, ROWS), :],
                    target.at[:, piece * width : (piece + 1) * width],
                    sems.at[2 + i * sizes.pieces + piece],
                )
            )
    for copy in copies:
        copy.start()
    copies[0].wait()
    for frame in range(sizes.frames):
        high, low = split_parts(latents_scr[frame])
        at = sizes.latents_at + 2 * frame * tokens
        payload_ref[:, at : at + tokens] = high
        payload_ref[:, at + tokens : at + 2 * tokens] = low
    copies[1].wait()
    for piece in range(sizes.text_pieces):
        first, last = piece * ROWS, min((piece + 1) * ROWS, sizes.part)
        at = sizes.text_at + piece * sizes.text_len
        for target, place in ((payload_ref, core), (mate_ref, 1 - core)):
            rows = text_scr[place, first:last, :]
            if last - first < ROWS:
                blank = jnp.zeros((ROWS - (last - first), sizes.text_len), BF16)
                rows = jnp.concatenate([rows, blank], axis=0)
            target[:, at : at + sizes.text_len] = rows
    tail_ref[...] = payload_ref[:, sizes.text_at :]
    for copy in copies[2:]:
        copy.wait()
    own_frame = lax.rem(lax.axis_index("seq"), sizes.frames)
    base = sizes.latents_at
    for d, near_ref in enumerate(near_refs, 1):
        near_ref[:, :base] = payload_ref[:, :base]
        at = base + 2 * tokens * jnp.bitwise_xor(own_frame, d)
        near_ref[:, base:] = payload_ref[:, pl.ds(pl.multiple_of(at, LANES), 2 * tokens)]


def join_kernel(sizes, far_ref, tail_ref, joined_ref):
    joined_ref[:, : sizes.payload] = far_ref[...]
    joined_ref[:, sizes.payload :] = tail_ref[...]


def frame_latents(sizes, mine_ref):
    if mine_ref.shape[1] == sizes.near:
        return mine_ref[:, sizes.latents_at :]
    frame = lax.rem(lax.axis_index("seq"), sizes.frames)
    at = pl.multiple_of(sizes.latents_at + 2 * frame * sizes.tokens, LANES)
    return mine_ref[:, pl.ds(at, 2 * sizes.tokens)]


def unpack(sizes, block, mine_ref, other_ref, position_scr, latents_scr):
    width, tokens = sizes.width, sizes.tokens
    core = lax.rem(lax.axis_index("queue"), 2)
    for ref, place in ((mine_ref, core), (other_ref, 1 - core)):
        for piece in range(sizes.pieces):
            start = pl.multiple_of(block * tokens + place * sizes.half + piece * ROWS, ROWS)
            position_scr[pl.ds(start, ROWS), :] = ref[:, piece * width : (piece + 1) * width]
    both = frame_latents(sizes, mine_ref)
    lanes = slice(block * tokens, (block + 1) * tokens)
    latents_scr[0:ROWS, lanes] = both[:, :tokens]
    latents_scr[ROWS : 2 * ROWS, lanes] = both[:, tokens:]


def unpack_text(sizes, shard, mine_ref, other_ref, base, text_scr):
    core = lax.rem(lax.axis_index("queue"), 2)
    for ref, place in ((mine_ref, core), (other_ref, 1 - core)):
        for piece in range(sizes.text_pieces):
            first, last = piece * ROWS, min((piece + 1) * ROWS, sizes.part)
            at = base + piece * sizes.text_len
            rows = ref[:, at : at + sizes.text_len].astype(F32)
            start = pl.multiple_of(shard * sizes.part + first, 8)
            text_scr[place, pl.ds(start, last - first), :] = rows[: last - first]


def normalize(values, scale, shift):
    center = values - jnp.mean(values, axis=-1, keepdims=True)
    variance = jnp.mean(center * center, axis=-1, keepdims=True)
    return (center * lax.rsqrt(variance + EPSILON) * scale + shift).astype(BF16)


def embed_blocks(sizes, blocks, position_scr, latents_scr, embed_ref, rows_ref, normed_scr, hidden):
    tokens = sizes.tokens
    embed = jnp.concatenate([embed_ref[...], embed_ref[...]], axis=0)
    embedded = dot(latents_scr[...], embed, TN)
    for block in range(blocks):
        rows = slice(block * tokens, (block + 1) * tokens)
        values = embedded[rows] + position_scr[rows, :].astype(F32)
        if hidden is not None:
            hidden[rows, :] = values
        normed_scr[rows, :] = normalize(values, rows_ref[1:2, :], rows_ref[0:1, :])


def head_sums(sizes):
    column = lax.broadcasted_iota(jnp.int32, (sizes.width, LANES), 0)
    first = lax.broadcasted_iota(jnp.int32, (sizes.width, LANES), 1) * sizes.head
    inside = (column >= first) & (column < first + sizes.head)
    return jnp.where(inside, 1.0, 0.0).astype(BF16)


def head_spread(sizes):
    column = lax.broadcasted_iota(jnp.int32, (LANES, sizes.width), 1)
    first = lax.broadcasted_iota(jnp.int32, (LANES, sizes.width), 0) * sizes.head
    inside = (column >= first) & (column < first + sizes.head)
    one = jnp.where(inside, 1.0, 0.0).astype(BF16)
    return jnp.concatenate([one, one], axis=0)


def spread(values, spread_matrix):
    high, low = split_parts(values)
    return dot(jnp.concatenate([high, low], axis=1), spread_matrix)


def norm_rows(sizes, source, target, gain, sums_matrix, spread_matrix, step=256):
    for start in range(0, source.shape[0], step):
        wide = source[start : start + step, :].astype(F32)
        squares = dot((wide * wide).astype(BF16), sums_matrix) * (1.0 / sizes.head)
        factor = spread(lax.rsqrt(squares + EPSILON), spread_matrix)
        target[start : start + step, :] = (wide * factor * gain).astype(BF16)


def project(normed_scr, weight_ref, first, last, out_ref, chunk=256):
    for start in range(first, last, chunk):
        end = min(start + chunk, last)
        out_ref[:, start - first : end - first] = dot(
            normed_scr[...], weight_ref[:, start:end]
        ).astype(BF16)


def window(first, last, width):
    start = first // LANES * LANES
    end = min(-(-last // LANES) * LANES, width)
    return start, end


def lane_mask(shape, first, last, axis=1):
    lane = lax.broadcasted_iota(jnp.int32, shape, axis)
    return (lane >= first) & (lane < last)


def keep(values, first, last, axis=1):
    inside = lane_mask(values.shape, first, last, axis)
    return jnp.where(inside, values, jnp.zeros_like(values))


def attend_self(sizes, q_ref, k_ref, v_ref, num_ref, sum_ref, fresh, q_step=512):
    queries, width = q_ref.shape
    keys = k_ref.shape[0]
    q_step = min(q_step, queries)
    for q_start in range(0, queries, q_step):
        rows = slice(q_start, q_start + q_step)
        sums = jnp.zeros((q_step, LANES), F32)
        pending = jnp.zeros((q_step, LANES), F32)
        for h in range(sizes.heads):
            first, last = h * sizes.head, (h + 1) * sizes.head
            start, end = window(first, last, width)
            span = (first - start, last - start)
            scores = dot(keep(q_ref[rows, start:end], *span), k_ref[:, start:end], NT)
            weights = jnp.exp2(scores).astype(BF16)
            v = keep(v_ref[:, start:end], *span)
            mark = lane_mask((keys, LANES), h, h + 1)
            if end - start == LANES:
                ones = jnp.where(mark, 1.0, 0.0).astype(BF16)
                both = dot(weights, jnp.concatenate([v, ones], axis=1))
                sums = sums + both[:, LANES:]
                pending = pending + both[:, :LANES]
            else:
                lead = jnp.where(mark, jnp.ones((), BF16), v[:, :LANES])
                both = dot(weights, jnp.concatenate([lead, v[:, LANES:]], axis=1))
                tops = lane_mask((q_step, LANES), 0, sizes.heads)
                left = both[:, :LANES]
                sums = sums + jnp.where(tops, left, 0.0)
                pending = pending + jnp.where(tops, 0.0, left)
            if last >= start + LANES:
                if fresh:
                    num_ref[rows, start : start + LANES] = pending
                else:
                    num_ref[rows, start : start + LANES] += pending
                wide = end - start > LANES
                pending = both[:, LANES:] if wide else jnp.zeros((q_step, LANES), F32)
        if fresh:
            sum_ref[rows, :] = sums
        else:
            sum_ref[rows, :] += sums


def attend_text(sizes, q_ref, k_scr, v_scr, num_ref, sum_ref, q_step=512):
    queries, width = q_ref.shape
    keys = k_scr.shape[1]
    for q_start in range(0, queries, q_step):
        rows = slice(q_start, q_start + q_step)
        sums = jnp.zeros((q_step, LANES), F32)
        pending, pending_at = None, None
        for pair in range(0, sizes.heads, 2):
            edges = [(pair + i) * sizes.head for i in range(3)]
            start, end = window(edges[0], edges[2], width)
            spans = [(edges[i] - start, edges[i + 1] - start) for i in range(2)]
            k = jnp.concatenate([keep(k_scr[start:end, :], *span, 0) for span in spans], axis=1)
            v = jnp.concatenate([keep(v_scr[start:end, :], *span, 0) for span in spans], axis=1)
            ones = [
                jnp.where(lane_mask((keys, LANES), h, h + 1), 1.0, 0.0).astype(BF16)
                for h in (pair, pair + 1)
            ]
            weights = jnp.exp2(dot(q_ref[rows, start:end], k)).astype(BF16)
            both = dot(weights, v, NT)
            sums = sums + dot(weights, jnp.concatenate(ones, axis=0))
            for at in range(start, end, LANES):
                part = both[:, at - start : at - start + LANES]
                if pending_at == at:
                    part = pending + part
                elif pending_at is not None and pending_at < at:
                    num_ref[rows, pending_at : pending_at + LANES] = pending
                pending, pending_at = part, at
        num_ref[rows, pending_at : pending_at + LANES] = pending
        sum_ref[rows, :] = sums


def first_kernel(
    sizes, step_ref, levels_ref, modulation_ref, q_gain_ref, k_gain_ref, mine, other, embed_ref, weight_ref,
    rows_ref, near_ref, q_ref, k_ref, v_ref, hidden_ref,
    position_scr, latents_scr, normed_scr, proj_scr, sems,
):
    width = sizes.width
    copies = []
    for i in range(3):
        columns = slice(i * width, (i + 1) * width)
        copies.append(
            pltpu.make_async_copy(
                weight_ref.at[:, columns], near_ref.at[:, columns], sems.at[i]
            )
        )
        copies[i].start()
    frame = lax.rem(lax.axis_index("seq"), sizes.frames)
    index = step_ref[frame]
    for i in range(5):
        row = modulation_ref[i, pl.ds(index, 1), :]
        rows_ref[i : i + 1, :] = row + 1.0 if i in (1, 4) else row
    factor = math.log2(math.e) / math.sqrt(sizes.head)
    for h in range(sizes.heads):
        rows_ref[5:6, h * sizes.head : (h + 1) * sizes.head] = q_gain_ref[...] * factor
        rows_ref[6:7, h * sizes.head : (h + 1) * sizes.head] = k_gain_ref[...]
    rows_ref[7:8, :] = jnp.full((1, width), levels_ref[index + 1] - levels_ref[index])
    unpack(sizes, 0, mine, other, position_scr, latents_scr)
    embed_blocks(
        sizes, 1, position_scr, latents_scr, embed_ref, rows_ref, normed_scr, hidden_ref
    )
    matrices = head_sums(sizes), head_spread(sizes)
    copies[0].wait()
    project(normed_scr, near_ref, 0, width, proj_scr)
    norm_rows(sizes, proj_scr, q_ref, rows_ref[5:6, :], *matrices)
    copies[1].wait()
    project(normed_scr, near_ref, width, 2 * width, proj_scr)
    norm_rows(sizes, proj_scr, k_ref, rows_ref[6:7, :], *matrices)
    copies[2].wait()
    project(normed_scr, near_ref, 2 * width, 3 * width, v_ref)


def own_kernel(sizes, *refs):
    count = sizes.frames - 1
    mine, other = refs[:count], refs[count : 2 * count]
    (
        embed_ref, rows_ref, weight_ref, q_one, k_one, v_one, hidden_one,
        q_ref, k_ref, v_ref, hidden_ref, position_scr, latents_scr, normed_scr, proj_scr,
    ) = refs[2 * count :]
    width, tokens = sizes.width, sizes.tokens
    for block in range(count):
        unpack(sizes, block, mine[block], other[block], position_scr, latents_scr)
    q_ref[:tokens, :] = q_one[...]
    k_ref[:tokens, :] = k_one[...]
    v_ref[:tokens, :] = v_one[...]
    hidden_ref[:tokens, :] = hidden_one[...]
    embed_blocks(
        sizes, count, position_scr, latents_scr, embed_ref, rows_ref, normed_scr,
        hidden_ref.at[tokens:, :],
    )
    project(normed_scr, weight_ref, 0, 2 * width, proj_scr)
    project(normed_scr, weight_ref, 2 * width, 3 * width, v_ref.at[tokens:, :])
    matrices = head_sums(sizes), head_spread(sizes)
    norm_rows(
        sizes, proj_scr.at[:, :width], q_ref.at[tokens:, :], rows_ref[5:6, :], *matrices
    )
    norm_rows(
        sizes, proj_scr.at[:, width:], k_ref.at[tokens:, :], rows_ref[6:7, :], *matrices
    )


def attend_kernel(sizes, q_ref, k_ref, v_ref, out_weight_ref, num_ref, sum_ref, near_ref, sem):
    copy = pltpu.make_async_copy(out_weight_ref, near_ref, sem)
    copy.start()
    attend_self(sizes, q_ref, k_ref, v_ref, num_ref, sum_ref, True)
    copy.wait()


def far_kernel(sizes, *refs):
    count, width = sizes.share - 1, sizes.width
    mine, other = refs[:count], refs[count : 2 * count]
    (
        embed_ref, rows_ref, weight_ref, k_ref, v_ref,
        position_scr, latents_scr, normed_scr, proj_scr,
    ) = refs[2 * count :]
    for block in range(count):
        unpack(sizes, block, mine[block], other[block], position_scr, latents_scr)
    embed_blocks(
        sizes, count, position_scr, latents_scr, embed_ref, rows_ref, normed_scr, None
    )
    project(normed_scr, weight_ref, width, 2 * width, proj_scr)
    norm_rows(sizes, proj_scr, k_ref, rows_ref[6:7, :], head_sums(sizes), head_spread(sizes))
    project(normed_scr, weight_ref, 2 * width, 3 * width, v_ref)


def rest_kernel(sizes, *refs):
    frames, share, width, tokens = sizes.frames, sizes.share, sizes.width, sizes.tokens
    count = frames * (share - 1)
    mine, other = refs[:count], refs[count : 2 * count]
    refs = refs[2 * count :]
    payload_ref, payload_other_ref = refs[:2]
    square = refs[2 : 1 + frames]
    (
        embed_ref, rows_ref, weight_ref, q_ref, hidden_ref, num_in_ref, sum_in_ref,
        out_weight_ref, final_weight_ref, far_k_ref, far_v_ref,
    ) = refs[1 + frames : 12 + frames]
    refs = refs[12 + frames :]
    velocity_refs = refs[:frames]
    updated_refs = refs[frames : 2 * frames]
    (
        position_scr, latents_scr, normed_scr, proj_scr, k_scr, v_scr, num_ref, sum_ref,
        text_scr, tk_scr, tv_scr, tnum_scr, tsum_scr, attention_scr,
    ) = refs[2 * frames :]
    sums_matrix, spread_matrix = head_sums(sizes), head_spread(sizes)
    num_ref[...] = num_in_ref[...]
    sum_ref[...] = sum_in_ref[...]
    for group in range(share - 1):
        first = slice(group * tokens, (group + 1) * tokens)
        k_scr[:tokens, :] = far_k_ref[first, :]
        v_scr[:tokens, :] = far_v_ref[first, :]
        for block in range(1, frames):
            at = group * frames + block
            unpack(sizes, block - 1, mine[at], other[at], position_scr, latents_scr)
        embed_blocks(
            sizes, frames - 1, position_scr, latents_scr, embed_ref, rows_ref, normed_scr, None
        )
        project(normed_scr, weight_ref, width, 2 * width, proj_scr)
        project(normed_scr, weight_ref, 2 * width, 3 * width, v_scr.at[tokens:, :])
        keys = k_scr.at[tokens:, :]
        norm_rows(sizes, proj_scr, keys, rows_ref[6:7, :], sums_matrix, spread_matrix)
        attend_self(sizes, q_ref, k_scr, v_scr, num_ref, sum_ref, False)

    place = lax.axis_index("seq")
    unpack_text(sizes, place, payload_ref, payload_other_ref, sizes.text_at, text_scr)
    for d in range(1, frames):
        shard = jnp.bitwise_xor(place, d)
        unpack_text(sizes, shard, mine[d], other[d], sizes.payload, text_scr)
    for at in range(count):
        shard = jnp.bitwise_xor(place, frames + at)
        unpack_text(sizes, shard, mine[at], other[at], sizes.text_at, text_scr)
    gain_column = jnp.transpose(jnp.broadcast_to(rows_ref[6:7, :], (LANES, width)))[:, 0:1]
    for h in range(sizes.heads):
        rows = slice(h * sizes.head, (h + 1) * sizes.head)
        values = text_scr[0, rows, :]
        mean = jnp.mean(values * values, axis=0, keepdims=True)
        text_scr[0, rows, :] = values * lax.rsqrt(mean + EPSILON) * gain_column[rows]
    tk_scr[...] = text_scr[0].astype(BF16)
    tv_scr[...] = text_scr[1].astype(BF16)
    attend_text(sizes, q_ref, tk_scr, tv_scr, tnum_scr, tsum_scr)

    for start in range(0, sizes.queries, LANES):
        rows = slice(start, start + LANES)
        used = lane_mask((LANES, LANES), 0, sizes.heads)
        own = spread(jnp.where(used, 1.0 / sum_ref[rows, :], 0.0), spread_matrix)
        text = spread(jnp.where(used, 1.0 / tsum_scr[rows, :], 0.0), spread_matrix)
        attention_scr[rows, :] = (num_ref[rows, :] * own + tnum_scr[rows, :] * text).astype(BF16)
    num_ref[...] = dot(attention_scr[...], out_weight_ref[...])
    for block in range(frames):
        rows = slice(block * tokens, (block + 1) * tokens)
        hidden = hidden_ref[rows, :] + rows_ref[2:3, :] * num_ref[rows, :]
        normed = normalize(hidden, rows_ref[4:5, :], rows_ref[3:4, :])
        velocity = dot(final_weight_ref[...], normed, NT)
        velocity_refs[block][...] = velocity
        both = frame_latents(sizes, square[block - 1] if block else payload_ref).astype(F32)
        before = both[:, :tokens] + both[:, tokens:]
        updated_refs[block][...] = before + rows_ref[7:8, :tokens] * velocity


def finish_kernel(sizes, step_ref, levels_ref, latents_ref, noise_ref, *refs):
    frames = sizes.frames
    arrived, next_ones = refs[:frames], refs[frames : 2 * frames]
    advanced_ref, velocity_ref = refs[2 * frames :]
    own_frame = lax.rem(lax.axis_index("seq"), frames)
    for d in range(frames):
        velocity_ref[jnp.bitwise_xor(own_frame, d)] = arrived[d][...]
    for frame in range(1, frames):
        index = step_ref[frame]
        size = levels_ref[index + 1] - levels_ref[index]
        advanced_ref[frame - 1] = latents_ref[frame] + size * velocity_ref[frame]
    after = next_ones[0][...]
    for d in range(1, frames):
        after = jnp.where(own_frame == d, next_ones[d][...], after)
    at_end = lax.axis_index("queue") == lax.axis_size("queue") - 1
    advanced_ref[frames - 1] = jnp.where(at_end, noise_ref[...], after)


def kernel(function, sizes, name, places, outs, scratch, us):
    spaces = {"v": pltpu.VMEM, "h": pltpu.HBM, "s": pltpu.SMEM}
    return pl.pallas_call(
        functools.partial(function, sizes),
        out_shape=outs,
        in_specs=[pl.BlockSpec(memory_space=spaces[place]) for place in places],
        out_specs=jax.tree.map(lambda _: pl.BlockSpec(memory_space=pltpu.VMEM), outs),
        scratch_shapes=scratch,
        compiler_params=pltpu.CompilerParams(vmem_limit_bytes=VMEM_LIMIT),
        cost_estimate=pl.CostEstimate(
            flops=int(us * 1e9), bytes_accessed=int(us * 1e6), transcendentals=0
        ),
        name=name,
    )


def body(
    latents,
    step_index,
    levels,
    modulation,
    embed_weight,
    position,
    qkv_weight,
    q_gain,
    k_gain,
    text_kv,
    out_weight,
    final_weight,
    new_noise,
):
    text = jnp.swapaxes(text_kv, 1, 2)
    modulation = jnp.swapaxes(modulation, 0, 1)
    sizes = Sizes(latents, position, text, q_gain, lax.axis_size("seq"))
    frames, width, tokens, queries = sizes.frames, sizes.width, sizes.tokens, sizes.queries
    queue = lax.axis_size("queue")

    def swapped(value, d):
        return lax.ppermute(value, "seq", [(i, i ^ d) for i in range(sizes.seq)])

    def over_cores(value):
        return lax.ppermute(value, "queue", [(i, i ^ 1) for i in range(queue)])

    far = functools.partial(pltpu.with_memory_space_constraint, memory_space=pltpu.HBM)

    payload, payload_other, tail, *near = kernel(
        prep_kernel,
        sizes,
        "prep",
        "hhh",
        [
            pltpu.VMEM((ROWS, sizes.payload), BF16),
            pltpu.VMEM((ROWS, sizes.payload), BF16),
            pltpu.VMEM((ROWS, sizes.payload - sizes.text_at), BF16),
        ]
        + [pltpu.VMEM((ROWS, sizes.near), BF16)] * (frames - 1),
        [
            pltpu.VMEM(latents.shape, F32),
            pltpu.VMEM(text.shape, BF16),
            pltpu.SemaphoreType.DMA((2 + 2 * sizes.pieces,)),
        ],
        1.5,
    )(far(position), far(latents), far(text))

    order = sorted(range(1, frames), key=lambda d: (d.bit_count() - 2 * (d >= frames // 2), d))
    sent = {d: swapped(near[d - 1], d) for d in order}
    direct = [sent[d] for d in range(1, frames)]
    direct += [swapped(payload, group * frames) for group in range(1, sizes.share)]

    def blocks(count):
        return [
            pltpu.VMEM((count * tokens, width), BF16),
            pltpu.VMEM((2 * ROWS, count * tokens), BF16),
            pltpu.VMEM((count * tokens, width), BF16),
        ]

    def token_arrays(count):
        rows = count * tokens
        return [pltpu.VMEM((rows, width), BF16)] * 3 + [pltpu.VMEM((rows, width), F32)]

    rows, near_qkv, *one = kernel(
        first_kernel,
        sizes,
        "first",
        "ssvvvvvvh",
        [pltpu.VMEM((8, width), F32), pltpu.VMEM(qkv_weight.shape, BF16)] + token_arrays(1),
        blocks(1) + [pltpu.VMEM((tokens, width), BF16), pltpu.SemaphoreType.DMA((3,))],
        4,
    )(
        step_index,
        levels,
        modulation,
        q_gain[None],
        k_gain[None],
        payload,
        payload_other,
        embed_weight,
        far(qkv_weight),
    )
    square, far_blocks = direct[: frames - 1], direct[frames - 1 :]
    rows, *square = lax.optimization_barrier((rows, *square))
    rows, *far_blocks = lax.optimization_barrier((rows, *far_blocks))
    square_other = [over_cores(value) for value in square]
    far_other = [over_cores(value) for value in far_blocks]
    joined = [
        kernel(
            join_kernel,
            sizes,
            "join",
            "vv",
            pltpu.VMEM((ROWS, 2 * sizes.payload - sizes.text_at), BF16),
            [],
            0.3,
        )(value, tail)
        for value in far_blocks
    ]
    forwarded = [[swapped(value, d) for d in range(1, frames)] for value in joined]
    forwarded = sum(forwarded, [])
    q_hat, k_hat, value, hidden = kernel(
        own_kernel,
        sizes,
        "own",
        "v" * (2 * (frames - 1) + 7),
        token_arrays(frames),
        blocks(frames - 1) + [pltpu.VMEM(((frames - 1) * tokens, 2 * width), BF16)],
        8,
    )(*square, *square_other, embed_weight, rows, near_qkv, *one)
    num, sums, near_out = kernel(
        attend_kernel,
        sizes,
        "attend",
        "vvvh",
        [
            pltpu.VMEM((queries, width), F32),
            pltpu.VMEM((queries, LANES), F32),
            pltpu.VMEM(out_weight.shape, BF16),
        ],
        [pltpu.SemaphoreType.DMA],
        5,
    )(q_hat, k_hat, value, far(out_weight))
    num, rows_late, *forwarded = lax.optimization_barrier((num, rows, *forwarded))
    forwarded_other = [over_cores(value) for value in forwarded]
    far_rows = (sizes.share - 1) * tokens
    far_k, far_v = kernel(
        far_kernel,
        sizes,
        "far",
        "v" * (2 * len(far_blocks) + 3),
        [pltpu.VMEM((far_rows, width), BF16)] * 2,
        blocks(sizes.share - 1) + [pltpu.VMEM((far_rows, width), BF16)],
        2.5,
    )(*far_blocks, *far_other, embed_weight, rows_late, near_qkv)
    mine, other = [], []
    for group in range(sizes.share - 1):
        here = slice(group * (frames - 1), (group + 1) * (frames - 1))
        mine += [far_blocks[group], *forwarded[here]]
        other += [far_other[group], *forwarded_other[here]]
    results = kernel(
        rest_kernel,
        sizes,
        "rest",
        "v" * (2 * len(mine) + 12 + frames),
        [pltpu.VMEM((sizes.channels, tokens), F32)] * (2 * frames),
        blocks(frames - 1)
        + [pltpu.VMEM(((frames - 1) * tokens, width), BF16)]
        + [pltpu.VMEM((queries, width), BF16)] * 2
        + [
            pltpu.VMEM((queries, width), F32),
            pltpu.VMEM((queries, LANES), F32),
            pltpu.VMEM((2, width, sizes.text_len), F32),
            pltpu.VMEM((width, sizes.text_len), BF16),
            pltpu.VMEM((width, sizes.text_len), BF16),
            pltpu.VMEM((queries, width), F32),
            pltpu.VMEM((queries, LANES), F32),
            pltpu.VMEM((queries, width), BF16),
        ],
        18,
    )(
        *mine,
        *other,
        payload,
        payload_other,
        *square,
        embed_weight,
        rows,
        near_qkv,
        q_hat,
        hidden,
        num,
        sums,
        near_out,
        final_weight.T,
        far_k,
        far_v,
    )

    velocities, updated = results[:frames], results[frames:]

    def to_previous(value, d):
        route = [
            (q * sizes.seq + i, (q - 1) * sizes.seq + (i ^ d))
            for q in range(1, queue)
            for i in range(0, sizes.seq, frames)
        ]
        return lax.ppermute(value, ("queue", "seq"), route)

    arrived = [velocities[0]] + [swapped(velocities[d], d) for d in range(1, frames)]
    next_ones = [to_previous(updated[d], d) for d in range(frames)]
    whole = jax.ShapeDtypeStruct(latents.shape, F32)
    return tuple(
        kernel(finish_kernel, sizes, "finish", "ss" + "v" * (2 + 2 * frames), [whole, whole], [], 1)(
            step_index, levels, latents, new_noise, *arrived, *next_ones
        )
    )


def solution(mesh):
    in_specs = (
        P("queue", None, "seq"),
        P("queue"),
        P(),
        P(),
        P(),
        P("seq", None),
        P(),
        P(),
        P(),
        P(None, None, "seq"),
        P(),
        P(),
        P(None, "seq"),
    )
    out_specs = (P("queue", None, "seq"), P("queue", None, "seq"))
    return jax.shard_map(body, mesh=mesh, in_specs=in_specs, out_specs=out_specs, check_vma=False)
```

```python
import functools
import math

import jax
import jax.numpy as jnp
from jax import lax
from jax.experimental import pallas as pl
from jax.experimental.pallas import tpu as pltpu
from jax.sharding import PartitionSpec as P

EPSILON = 1e-06
LANES = 128
ROWS = 16
F32 = jnp.float32
BF16 = jnp.bfloat16
VMEM_LIMIT = 24 * 1024 * 1024
NN = (((1,), (0,)), ((), ()))
NT = (((1,), (1,)), ((), ()))
TN = (((0,), (0,)), ((), ()))


def dot(a, b, dims=NN):
    return lax.dot_general(a, b, dims, preferred_element_type=F32)


def split_parts(values):
    high = values.astype(BF16)
    low = (values - high.astype(F32)).astype(BF16)
    return high, low


class Sizes:
    def __init__(self, latents, position, text, q_gain, seq):
        self.frames, self.channels, self.tokens = latents.shape
        self.width = position.shape[1]
        self.head = q_gain.shape[0]
        self.heads = self.width // self.head
        self.seq = seq
        self.share = seq // self.frames
        self.queries = self.frames * self.tokens
        _, self.part, self.text_len = text.shape
        self.half = self.tokens // 2
        self.pieces = self.half // ROWS
        self.text_pieces = -(-self.part // ROWS)
        self.latents_at = self.pieces * self.width
        self.text_at = self.latents_at + 2 * self.frames * self.tokens
        self.payload = self.text_at + self.text_pieces * self.text_len
        self.near = self.latents_at + 2 * self.tokens


def prep_kernel(sizes, position_ref, latents_ref, text_ref, payload_ref, mate_ref, tail_ref, *refs):
    near_refs, (latents_scr, text_scr, sems) = refs[:-3], refs[-3:]
    core = lax.rem(lax.axis_index("queue"), 2)
    width, tokens = sizes.width, sizes.tokens
    copies = [
        pltpu.make_async_copy(latents_ref, latents_scr, sems.at[0]),
        pltpu.make_async_copy(text_ref, text_scr, sems.at[1]),
    ]
    for i, (target, place) in enumerate(((payload_ref, core), (mate_ref, 1 - core))):
        for piece in range(sizes.pieces):
            start = pl.multiple_of(place * sizes.half + piece * ROWS, ROWS)
            copies.append(
                pltpu.make_async_copy(
                    position_ref.at[pl.ds(start, ROWS), :],
                    target.at[:, piece * width : (piece + 1) * width],
                    sems.at[2 + i * sizes.pieces + piece],
                )
            )
    for copy in copies:
        copy.start()
    copies[0].wait()
    for frame in range(sizes.frames):
        high, low = split_parts(latents_scr[frame])
        at = sizes.latents_at + 2 * frame * tokens
        payload_ref[:, at : at + tokens] = high
        payload_ref[:, at + tokens : at + 2 * tokens] = low
    copies[1].wait()
    for piece in range(sizes.text_pieces):
        first, last = piece * ROWS, min((piece + 1) * ROWS, sizes.part)
        at = sizes.text_at + piece * sizes.text_len
        for target, place in ((payload_ref, core), (mate_ref, 1 - core)):
            rows = text_scr[place, first:last, :]
            if last - first < ROWS:
                blank = jnp.zeros((ROWS - (last - first), sizes.text_len), BF16)
                rows = jnp.concatenate([rows, blank], axis=0)
            target[:, at : at + sizes.text_len] = rows
    tail_ref[...] = payload_ref[:, sizes.text_at :]
    for copy in copies[2:]:
        copy.wait()
    own_frame = lax.rem(lax.axis_index("seq"), sizes.frames)
    base = sizes.latents_at
    for d, near_ref in enumerate(near_refs, 1):
        near_ref[:, :base] = payload_ref[:, :base]
        at = base + 2 * tokens * jnp.bitwise_xor(own_frame, d)
        near_ref[:, base:] = payload_ref[:, pl.ds(pl.multiple_of(at, LANES), 2 * tokens)]


def join_kernel(sizes, far_ref, tail_ref, joined_ref):
    joined_ref[:, : sizes.payload] = far_ref[...]
    joined_ref[:, sizes.payload :] = tail_ref[...]


def frame_latents(sizes, mine_ref):
    if mine_ref.shape[1] == sizes.near:
        return mine_ref[:, sizes.latents_at :]
    frame = lax.rem(lax.axis_index("seq"), sizes.frames)
    at = pl.multiple_of(sizes.latents_at + 2 * frame * sizes.tokens, LANES)
    return mine_ref[:, pl.ds(at, 2 * sizes.tokens)]


def unpack(sizes, block, mine_ref, other_ref, position_scr, latents_scr):
    width, tokens = sizes.width, sizes.tokens
    core = lax.rem(lax.axis_index("queue"), 2)
    for ref, place in ((mine_ref, core), (other_ref, 1 - core)):
        for piece in range(sizes.pieces):
            start = pl.multiple_of(block * tokens + place * sizes.half + piece * ROWS, ROWS)
            position_scr[pl.ds(start, ROWS), :] = ref[:, piece * width : (piece + 1) * width]
    both = frame_latents(sizes, mine_ref)
    lanes = slice(block * tokens, (block + 1) * tokens)
    latents_scr[0:ROWS, lanes] = both[:, :tokens]
    latents_scr[ROWS : 2 * ROWS, lanes] = both[:, tokens:]


def unpack_text(sizes, shard, mine_ref, other_ref, base, text_scr):
    core = lax.rem(lax.axis_index("queue"), 2)
    for ref, place in ((mine_ref, core), (other_ref, 1 - core)):
        for piece in range(sizes.text_pieces):
            first, last = piece * ROWS, min((piece + 1) * ROWS, sizes.part)
            at = base + piece * sizes.text_len
            rows = ref[:, at : at + sizes.text_len].astype(F32)
            start = pl.multiple_of(shard * sizes.part + first, 8)
            text_scr[place, pl.ds(start, last - first), :] = rows[: last - first]


def normalize(values, scale, shift):
    center = values - jnp.mean(values, axis=-1, keepdims=True)
    variance = jnp.mean(center * center, axis=-1, keepdims=True)
    return (center * lax.rsqrt(variance + EPSILON) * scale + shift).astype(BF16)


def embed_blocks(sizes, blocks, position_scr, latents_scr, embed_ref, rows_ref, normed_scr, hidden):
    tokens = sizes.tokens
    embed = jnp.concatenate([embed_ref[...], embed_ref[...]], axis=0)
    embedded = dot(latents_scr[...], embed, TN)
    for block in range(blocks):
        rows = slice(block * tokens, (block + 1) * tokens)
        values = embedded[rows] + position_scr[rows, :].astype(F32)
        if hidden is not None:
            hidden[rows, :] = values
        normed_scr[rows, :] = normalize(values, rows_ref[1:2, :], rows_ref[0:1, :])


def head_sums(sizes):
    column = lax.broadcasted_iota(jnp.int32, (sizes.width, LANES), 0)
    first = lax.broadcasted_iota(jnp.int32, (sizes.width, LANES), 1) * sizes.head
    inside = (column >= first) & (column < first + sizes.head)
    return jnp.where(inside, 1.0, 0.0).astype(BF16)


def head_spread(sizes):
    column = lax.broadcasted_iota(jnp.int32, (LANES, sizes.width), 1)
    first = lax.broadcasted_iota(jnp.int32, (LANES, sizes.width), 0) * sizes.head
    inside = (column >= first) & (column < first + sizes.head)
    one = jnp.where(inside, 1.0, 0.0).astype(BF16)
    return jnp.concatenate([one, one], axis=0)


def spread(values, spread_matrix):
    high, low = split_parts(values)
    return dot(jnp.concatenate([high, low], axis=1), spread_matrix)


def norm_rows(sizes, source, target, gain, sums_matrix, spread_matrix, step=256):
    for start in range(0, source.shape[0], step):
        wide = source[start : start + step, :].astype(F32)
        squares = dot((wide * wide).astype(BF16), sums_matrix) * (1.0 / sizes.head)
        factor = spread(lax.rsqrt(squares + EPSILON), spread_matrix)
        target[start : start + step, :] = (wide * factor * gain).astype(BF16)


def project(normed_scr, weight_ref, first, last, out_ref, chunk=256):
    for start in range(first, last, chunk):
        end = min(start + chunk, last)
        out_ref[:, start - first : end - first] = dot(
            normed_scr[...], weight_ref[:, start:end]
        ).astype(BF16)


def window(first, last, width):
    start = first // LANES * LANES
    end = min(-(-last // LANES) * LANES, width)
    return start, end


def lane_mask(shape, first, last, axis=1):
    lane = lax.broadcasted_iota(jnp.int32, shape, axis)
    return (lane >= first) & (lane < last)


def keep(values, first, last, axis=1):
    inside = lane_mask(values.shape, first, last, axis)
    return jnp.where(inside, values, jnp.zeros_like(values))


def attend_self(sizes, q_ref, k_ref, v_ref, num_ref, sum_ref, before, q_step=512):
    queries, width = q_ref.shape
    keys = k_ref.shape[0]
    q_step = min(q_step, queries)
    for q_start in range(0, queries, q_step):
        rows = slice(q_start, q_start + q_step)
        sums = jnp.zeros((q_step, LANES), F32)
        pending = jnp.zeros((q_step, LANES), F32)
        for h in range(sizes.heads):
            first, last = h * sizes.head, (h + 1) * sizes.head
            start, end = window(first, last, width)
            span = (first - start, last - start)
            scores = dot(keep(q_ref[rows, start:end], *span), k_ref[:, start:end], NT)
            weights = jnp.exp2(scores).astype(BF16)
            v = keep(v_ref[:, start:end], *span)
            mark = lane_mask((keys, LANES), h, h + 1)
            if end - start == LANES:
                ones = jnp.where(mark, 1.0, 0.0).astype(BF16)
                both = dot(weights, jnp.concatenate([v, ones], axis=1))
                sums = sums + both[:, LANES:]
                pending = pending + both[:, :LANES]
            else:
                lead = jnp.where(mark, jnp.ones((), BF16), v[:, :LANES])
                both = dot(weights, jnp.concatenate([lead, v[:, LANES:]], axis=1))
                tops = lane_mask((q_step, LANES), 0, sizes.heads)
                left = both[:, :LANES]
                sums = sums + jnp.where(tops, left, 0.0)
                pending = pending + jnp.where(tops, 0.0, left)
            if last >= start + LANES:
                columns = slice(start, start + LANES)
                if before is not None:
                    pending = before[0][rows, columns] + pending
                num_ref[rows, columns] = pending
                wide = end - start > LANES
                pending = both[:, LANES:] if wide else jnp.zeros((q_step, LANES), F32)
        sum_ref[rows, :] = sums if before is None else before[1][rows, :] + sums


def attend_text(sizes, q_ref, k_scr, v_scr, num_ref, sum_ref, q_step=512):
    queries, width = q_ref.shape
    keys = k_scr.shape[1]
    for q_start in range(0, queries, q_step):
        rows = slice(q_start, q_start + q_step)
        sums = jnp.zeros((q_step, LANES), F32)
        pending, pending_at = None, None
        for pair in range(0, sizes.heads, 2):
            edges = [(pair + i) * sizes.head for i in range(3)]
            start, end = window(edges[0], edges[2], width)
            spans = [(edges[i] - start, edges[i + 1] - start) for i in range(2)]
            k = jnp.concatenate([keep(k_scr[start:end, :], *span, 0) for span in spans], axis=1)
            v = jnp.concatenate([keep(v_scr[start:end, :], *span, 0) for span in spans], axis=1)
            ones = [
                jnp.where(lane_mask((keys, LANES), h, h + 1), 1.0, 0.0).astype(BF16)
                for h in (pair, pair + 1)
            ]
            weights = jnp.exp2(dot(q_ref[rows, start:end], k)).astype(BF16)
            both = dot(weights, v, NT)
            sums = sums + dot(weights, jnp.concatenate(ones, axis=0))
            for at in range(start, end, LANES):
                part = both[:, at - start : at - start + LANES]
                if pending_at == at:
                    part = pending + part
                elif pending_at is not None and pending_at < at:
                    num_ref[rows, pending_at : pending_at + LANES] = pending
                pending, pending_at = part, at
        num_ref[rows, pending_at : pending_at + LANES] = pending
        sum_ref[rows, :] = sums


def first_kernel(
    sizes, step_ref, levels_ref, modulation_ref, q_gain_ref, k_gain_ref, mine, other, embed_ref, weight_ref,
    rows_ref, near_ref, q_ref, k_ref, v_ref, hidden_ref,
    position_scr, latents_scr, normed_scr, proj_scr, sems,
):
    width = sizes.width
    copies = []
    for i in range(3):
        columns = slice(i * width, (i + 1) * width)
        copies.append(
            pltpu.make_async_copy(
                weight_ref.at[:, columns], near_ref.at[:, columns], sems.at[i]
            )
        )
        copies[i].start()
    frame = lax.rem(lax.axis_index("seq"), sizes.frames)
    index = step_ref[frame]
    for i in range(5):
        row = modulation_ref[i, pl.ds(index, 1), :]
        rows_ref[i : i + 1, :] = row + 1.0 if i in (1, 4) else row
    factor = math.log2(math.e) / math.sqrt(sizes.head)
    for h in range(sizes.heads):
        rows_ref[5:6, h * sizes.head : (h + 1) * sizes.head] = q_gain_ref[...] * factor
        rows_ref[6:7, h * sizes.head : (h + 1) * sizes.head] = k_gain_ref[...]
    rows_ref[7:8, :] = jnp.full((1, width), levels_ref[index + 1] - levels_ref[index])
    unpack(sizes, 0, mine, other, position_scr, latents_scr)
    embed_blocks(
        sizes, 1, position_scr, latents_scr, embed_ref, rows_ref, normed_scr, hidden_ref
    )
    matrices = head_sums(sizes), head_spread(sizes)
    copies[0].wait()
    project(normed_scr, near_ref, 0, width, proj_scr)
    norm_rows(sizes, proj_scr, q_ref, rows_ref[5:6, :], *matrices)
    copies[1].wait()
    project(normed_scr, near_ref, width, 2 * width, proj_scr)
    norm_rows(sizes, proj_scr, k_ref, rows_ref[6:7, :], *matrices)
    copies[2].wait()
    project(normed_scr, near_ref, 2 * width, 3 * width, v_ref)


def own_kernel(sizes, *refs):
    count = sizes.frames - 1
    mine, other = refs[:count], refs[count : 2 * count]
    (
        embed_ref, rows_ref, weight_ref, q_one, k_one, v_one, hidden_one,
        q_ref, k_ref, v_ref, hidden_ref, position_scr, latents_scr, normed_scr, proj_scr,
    ) = refs[2 * count :]
    width, tokens = sizes.width, sizes.tokens
    for block in range(count):
        unpack(sizes, block, mine[block], other[block], position_scr, latents_scr)
    q_ref[:tokens, :] = q_one[...]
    k_ref[:tokens, :] = k_one[...]
    v_ref[:tokens, :] = v_one[...]
    hidden_ref[:tokens, :] = hidden_one[...]
    embed_blocks(
        sizes, count, position_scr, latents_scr, embed_ref, rows_ref, normed_scr,
        hidden_ref.at[tokens:, :],
    )
    project(normed_scr, weight_ref, 0, 2 * width, proj_scr)
    project(normed_scr, weight_ref, 2 * width, 3 * width, v_ref.at[tokens:, :])
    matrices = head_sums(sizes), head_spread(sizes)
    norm_rows(
        sizes, proj_scr.at[:, :width], q_ref.at[tokens:, :], rows_ref[5:6, :], *matrices
    )
    norm_rows(
        sizes, proj_scr.at[:, width:], k_ref.at[tokens:, :], rows_ref[6:7, :], *matrices
    )


def attend_kernel(sizes, q_ref, k_ref, v_ref, out_weight_ref, num_ref, sum_ref, near_ref, sem):
    copy = pltpu.make_async_copy(out_weight_ref, near_ref, sem)
    copy.start()
    attend_self(sizes, q_ref, k_ref, v_ref, num_ref, sum_ref, None)
    copy.wait()


def far_kernel(sizes, *refs):
    count, width = sizes.share - 1, sizes.width
    mine, other = refs[:count], refs[count : 2 * count]
    (
        embed_ref, rows_ref, weight_ref, k_ref, v_ref,
        position_scr, latents_scr, normed_scr, proj_scr,
    ) = refs[2 * count :]
    for block in range(count):
        unpack(sizes, block, mine[block], other[block], position_scr, latents_scr)
    embed_blocks(
        sizes, count, position_scr, latents_scr, embed_ref, rows_ref, normed_scr, None
    )
    project(normed_scr, weight_ref, width, 2 * width, proj_scr)
    norm_rows(sizes, proj_scr, k_ref, rows_ref[6:7, :], head_sums(sizes), head_spread(sizes))
    project(normed_scr, weight_ref, 2 * width, 3 * width, v_ref)


def rest_kernel(sizes, *refs):
    frames, share, width, tokens = sizes.frames, sizes.share, sizes.width, sizes.tokens
    count = frames * (share - 1)
    mine, other = refs[:count], refs[count : 2 * count]
    refs = refs[2 * count :]
    payload_ref, payload_other_ref = refs[:2]
    square = refs[2 : 1 + frames]
    (
        embed_ref, rows_ref, weight_ref, q_ref, hidden_ref, num_in_ref, sum_in_ref,
        out_weight_ref, final_weight_ref, far_k_ref, far_v_ref,
    ) = refs[1 + frames : 12 + frames]
    refs = refs[12 + frames :]
    velocity_refs = refs[:frames]
    updated_refs = refs[frames : 2 * frames]
    (
        position_scr, latents_scr, normed_scr, proj_scr, k_scr, v_scr, num_ref, sum_ref,
        text_scr, tk_scr, tv_scr, tnum_scr, tsum_scr, attention_scr,
    ) = refs[2 * frames :]
    sums_matrix, spread_matrix = head_sums(sizes), head_spread(sizes)
    before = num_in_ref, sum_in_ref
    for group in range(share - 1):
        first = slice(group * tokens, (group + 1) * tokens)
        k_scr[:tokens, :] = far_k_ref[first, :]
        v_scr[:tokens, :] = far_v_ref[first, :]
        for block in range(1, frames):
            at = group * frames + block
            unpack(sizes, block - 1, mine[at], other[at], position_scr, latents_scr)
        embed_blocks(
            sizes, frames - 1, position_scr, latents_scr, embed_ref, rows_ref, normed_scr, None
        )
        project(normed_scr, weight_ref, width, 2 * width, proj_scr)
        project(normed_scr, weight_ref, 2 * width, 3 * width, v_scr.at[tokens:, :])
        keys = k_scr.at[tokens:, :]
        norm_rows(sizes, proj_scr, keys, rows_ref[6:7, :], sums_matrix, spread_matrix)
        attend_self(sizes, q_ref, k_scr, v_scr, num_ref, sum_ref, before)
        before = num_ref, sum_ref

    place = lax.axis_index("seq")
    unpack_text(sizes, place, payload_ref, payload_other_ref, sizes.text_at, text_scr)
    for d in range(1, frames):
        shard = jnp.bitwise_xor(place, d)
        unpack_text(sizes, shard, mine[d], other[d], sizes.payload, text_scr)
    for at in range(count):
        shard = jnp.bitwise_xor(place, frames + at)
        unpack_text(sizes, shard, mine[at], other[at], sizes.text_at, text_scr)
    gain_column = jnp.transpose(jnp.broadcast_to(rows_ref[6:7, :], (LANES, width)))[:, 0:1]
    for h in range(sizes.heads):
        rows = slice(h * sizes.head, (h + 1) * sizes.head)
        values = text_scr[0, rows, :]
        mean = jnp.mean(values * values, axis=0, keepdims=True)
        text_scr[0, rows, :] = values * lax.rsqrt(mean + EPSILON) * gain_column[rows]
    tk_scr[...] = text_scr[0].astype(BF16)
    tv_scr[...] = text_scr[1].astype(BF16)
    attend_text(sizes, q_ref, tk_scr, tv_scr, tnum_scr, tsum_scr)

    step = 2 * LANES
    for start in range(0, sizes.queries, step):
        rows = slice(start, start + step)
        used = lane_mask((step, LANES), 0, sizes.heads)
        own = spread(jnp.where(used, 1.0 / sum_ref[rows, :], 0.0), spread_matrix)
        text = spread(jnp.where(used, 1.0 / tsum_scr[rows, :], 0.0), spread_matrix)
        attention_scr[rows, :] = (num_ref[rows, :] * own + tnum_scr[rows, :] * text).astype(BF16)
    num_ref[...] = dot(attention_scr[...], out_weight_ref[...])
    for block in range(frames):
        rows = slice(block * tokens, (block + 1) * tokens)
        hidden = hidden_ref[rows, :] + rows_ref[2:3, :] * num_ref[rows, :]
        normed = normalize(hidden, rows_ref[4:5, :], rows_ref[3:4, :])
        velocity = dot(final_weight_ref[...], normed, NT)
        velocity_refs[block][...] = velocity
        both = frame_latents(sizes, square[block - 1] if block else payload_ref).astype(F32)
        before = both[:, :tokens] + both[:, tokens:]
        updated_refs[block][...] = before + rows_ref[7:8, :tokens] * velocity


def finish_kernel(sizes, step_ref, levels_ref, latents_ref, noise_ref, *refs):
    frames = sizes.frames
    arrived, next_ones = refs[:frames], refs[frames : 2 * frames]
    advanced_ref, velocity_ref = refs[2 * frames :]
    own_frame = lax.rem(lax.axis_index("seq"), frames)
    for d in range(frames):
        velocity_ref[jnp.bitwise_xor(own_frame, d)] = arrived[d][...]
    for frame in range(1, frames):
        index = step_ref[frame]
        size = levels_ref[index + 1] - levels_ref[index]
        advanced_ref[frame - 1] = latents_ref[frame] + size * velocity_ref[frame]
    after = next_ones[0][...]
    for d in range(1, frames):
        after = jnp.where(own_frame == d, next_ones[d][...], after)
    at_end = lax.axis_index("queue") == lax.axis_size("queue") - 1
    advanced_ref[frames - 1] = jnp.where(at_end, noise_ref[...], after)


def kernel(function, sizes, name, places, outs, scratch, us):
    spaces = {"v": pltpu.VMEM, "h": pltpu.HBM, "s": pltpu.SMEM}
    return pl.pallas_call(
        functools.partial(function, sizes),
        out_shape=outs,
        in_specs=[pl.BlockSpec(memory_space=spaces[place]) for place in places],
        out_specs=jax.tree.map(lambda _: pl.BlockSpec(memory_space=pltpu.VMEM), outs),
        scratch_shapes=scratch,
        compiler_params=pltpu.CompilerParams(vmem_limit_bytes=VMEM_LIMIT),
        cost_estimate=pl.CostEstimate(
            flops=int(us * 1e9), bytes_accessed=int(us * 1e6), transcendentals=0
        ),
        name=name,
    )


def body(
    latents,
    step_index,
    levels,
    modulation,
    embed_weight,
    position,
    qkv_weight,
    q_gain,
    k_gain,
    text_kv,
    out_weight,
    final_weight,
    new_noise,
):
    text = jnp.swapaxes(text_kv, 1, 2)
    modulation = jnp.swapaxes(modulation, 0, 1)
    sizes = Sizes(latents, position, text, q_gain, lax.axis_size("seq"))
    frames, width, tokens, queries = sizes.frames, sizes.width, sizes.tokens, sizes.queries
    queue = lax.axis_size("queue")

    def swapped(value, d):
        return lax.ppermute(value, "seq", [(i, i ^ d) for i in range(sizes.seq)])

    def over_cores(value):
        return lax.ppermute(value, "queue", [(i, i ^ 1) for i in range(queue)])

    far = functools.partial(pltpu.with_memory_space_constraint, memory_space=pltpu.HBM)

    payload, payload_other, tail, *near = kernel(
        prep_kernel,
        sizes,
        "prep",
        "hhh",
        [
            pltpu.VMEM((ROWS, sizes.payload), BF16),
            pltpu.VMEM((ROWS, sizes.payload), BF16),
            pltpu.VMEM((ROWS, sizes.payload - sizes.text_at), BF16),
        ]
        + [pltpu.VMEM((ROWS, sizes.near), BF16)] * (frames - 1),
        [
            pltpu.VMEM(latents.shape, F32),
            pltpu.VMEM(text.shape, BF16),
            pltpu.SemaphoreType.DMA((2 + 2 * sizes.pieces,)),
        ],
        1.5,
    )(far(position), far(latents), far(text))

    order = sorted(range(1, frames), key=lambda d: (d.bit_count() - 2 * (d >= frames // 2), d))
    sent = {d: swapped(near[d - 1], d) for d in order}
    direct = [sent[d] for d in range(1, frames)]
    direct += [swapped(payload, group * frames) for group in range(1, sizes.share)]

    def blocks(count):
        return [
            pltpu.VMEM((count * tokens, width), BF16),
            pltpu.VMEM((2 * ROWS, count * tokens), BF16),
            pltpu.VMEM((count * tokens, width), BF16),
        ]

    def token_arrays(count):
        rows = count * tokens
        return [pltpu.VMEM((rows, width), BF16)] * 3 + [pltpu.VMEM((rows, width), F32)]

    rows, near_qkv, *one = kernel(
        first_kernel,
        sizes,
        "first",
        "ssvvvvvvh",
        [pltpu.VMEM((8, width), F32), pltpu.VMEM(qkv_weight.shape, BF16)] + token_arrays(1),
        blocks(1) + [pltpu.VMEM((tokens, width), BF16), pltpu.SemaphoreType.DMA((3,))],
        4,
    )(
        step_index,
        levels,
        modulation,
        q_gain[None],
        k_gain[None],
        payload,
        payload_other,
        embed_weight,
        far(qkv_weight),
    )
    square, far_blocks = direct[: frames - 1], direct[frames - 1 :]
    rows, *square = lax.optimization_barrier((rows, *square))
    rows, *far_blocks = lax.optimization_barrier((rows, *far_blocks))
    square_other = [over_cores(value) for value in square]
    far_other = [over_cores(value) for value in far_blocks]
    joined = [
        kernel(
            join_kernel,
            sizes,
            "join",
            "vv",
            pltpu.VMEM((ROWS, 2 * sizes.payload - sizes.text_at), BF16),
            [],
            0.3,
        )(value, tail)
        for value in far_blocks
    ]
    forwarded = [[swapped(value, d) for d in range(1, frames)] for value in joined]
    forwarded = sum(forwarded, [])
    q_hat, k_hat, value, hidden = kernel(
        own_kernel,
        sizes,
        "own",
        "v" * (2 * (frames - 1) + 7),
        token_arrays(frames),
        blocks(frames - 1) + [pltpu.VMEM(((frames - 1) * tokens, 2 * width), BF16)],
        8,
    )(*square, *square_other, embed_weight, rows, near_qkv, *one)
    num, sums, near_out = kernel(
        attend_kernel,
        sizes,
        "attend",
        "vvvh",
        [
            pltpu.VMEM((queries, width), F32),
            pltpu.VMEM((queries, LANES), F32),
            pltpu.VMEM(out_weight.shape, BF16),
        ],
        [pltpu.SemaphoreType.DMA],
        5,
    )(q_hat, k_hat, value, far(out_weight))
    num, rows_late, *forwarded = lax.optimization_barrier((num, rows, *forwarded))
    forwarded_other = [over_cores(value) for value in forwarded]
    far_rows = (sizes.share - 1) * tokens
    far_k, far_v = kernel(
        far_kernel,
        sizes,
        "far",
        "v" * (2 * len(far_blocks) + 3),
        [pltpu.VMEM((far_rows, width), BF16)] * 2,
        blocks(sizes.share - 1) + [pltpu.VMEM((far_rows, width), BF16)],
        2.5,
    )(*far_blocks, *far_other, embed_weight, rows_late, near_qkv)
    mine, other = [], []
    for group in range(sizes.share - 1):
        here = slice(group * (frames - 1), (group + 1) * (frames - 1))
        mine += [far_blocks[group], *forwarded[here]]
        other += [far_other[group], *forwarded_other[here]]
    results = kernel(
        rest_kernel,
        sizes,
        "rest",
        "v" * (2 * len(mine) + 12 + frames),
        [pltpu.VMEM((sizes.channels, tokens), F32)] * (2 * frames),
        blocks(frames - 1)
        + [pltpu.VMEM(((frames - 1) * tokens, width), BF16)]
        + [pltpu.VMEM((queries, width), BF16)] * 2
        + [
            pltpu.VMEM((queries, width), F32),
            pltpu.VMEM((queries, LANES), F32),
            pltpu.VMEM((2, width, sizes.text_len), F32),
            pltpu.VMEM((width, sizes.text_len), BF16),
            pltpu.VMEM((width, sizes.text_len), BF16),
            pltpu.VMEM((queries, width), F32),
            pltpu.VMEM((queries, LANES), F32),
            pltpu.VMEM((queries, width), BF16),
        ],
        18,
    )(
        *mine,
        *other,
        payload,
        payload_other,
        *square,
        embed_weight,
        rows,
        near_qkv,
        q_hat,
        hidden,
        num,
        sums,
        near_out,
        final_weight.T,
        far_k,
        far_v,
    )

    velocities, updated = results[:frames], results[frames:]

    def to_previous(value, d):
        route = [
            (q * sizes.seq + i, (q - 1) * sizes.seq + (i ^ d))
            for q in range(1, queue)
            for i in range(0, sizes.seq, frames)
        ]
        return lax.ppermute(value, ("queue", "seq"), route)

    arrived = [velocities[0]] + [swapped(velocities[d], d) for d in range(1, frames)]
    next_ones = [to_previous(updated[d], d) for d in range(frames)]
    whole = jax.ShapeDtypeStruct(latents.shape, F32)
    return tuple(
        kernel(finish_kernel, sizes, "finish", "ss" + "v" * (2 + 2 * frames), [whole, whole], [], 1)(
            step_index, levels, latents, new_noise, *arrived, *next_ones
        )
    )


def solution(mesh):
    in_specs = (
        P("queue", None, "seq"),
        P("queue"),
        P(),
        P(),
        P(),
        P("seq", None),
        P(),
        P(),
        P(),
        P(None, None, "seq"),
        P(),
        P(),
        P(None, "seq"),
    )
    out_specs = (P("queue", None, "seq"), P("queue", None, "seq"))
    return jax.shard_map(body, mesh=mesh, in_specs=in_specs, out_specs=out_specs, check_vma=False)
```
